256 devices in a mesh: lat: 32 (over x, z), member: 8 (over y, core).
Axes of the slice: x: 4, y: 4, z: 8, core: 2. Of those that a mesh axis runs over, the one named last changes fastest.
Arguments:
- frames: bfloat16 [8, 256, 512, 128], P('member', 'lat'), may hold values from -6 to 6
- window: int32 [8], replicated, may hold values from 0 to 7, as said below
- targets: bfloat16 [8, 256, 512, 128], P('member', 'lat'), may hold values from -1.5 to 1.5
- w_in: bfloat16 [8, 128, 256], P('member'), may hold values from -0.5 to 0.5
- w_out: bfloat16 [8, 256, 128], P('member'), may hold values from -0.375 to 0.375
- legendre: bfloat16 [256, 256, 256], P('lat'), as said below
- damping: float32 [256], replicated, may hold values from 0.2 to 0.6
Outputs:
- grad_in: float32 [8, 128, 256], P('member')
- grad_out: float32 [8, 256, 128], P('member')
The draws below stay inside these ranges and needn't reach their ends.
Inputs may be any that keep to these rules, and one draw needn't show every extreme that they name: window[k] // 1 differs for every member k. legendre[m, a, l] is zero for l < m.
All inputs are finite; a program needn't handle non-finite values.
Results may differ from the reference program's by a relative error of at most 0.0011.
Values may be sent and summed in bfloat16 or wider, within the bound.
No kernel may reach another device: no remote copies, remote signals or barrier semaphores. Data moves between devices by JAX's collectives and lax.ppermute only.
A program may use at most 128 MiB of HBM per device.

```python
import math
import jax
import jax.numpy as jnp
from jax import lax

LAT = 256
LON = 512
MW = 256
L = 256
CH = 128
HID = 256
STEPS = 3
FR_DEV = 1
MEMBERS = 8
FRAMES = 8


def place_owner(owners, position, wanted):
    where_now = jnp.argmax((owners == wanted).astype(jnp.int32)).astype(jnp.int32)
    held = owners[position]
    owners = owners.at[where_now].set(held)
    return owners.at[position].set(wanted)


def draw_window(key, part):
    key = jax.random.fold_in(key, 7)
    first_key, second_key = jax.random.split(key)
    owners = jax.random.permutation(first_key, MEMBERS).astype(jnp.int32)
    owners = place_owner(owners, 0, MEMBERS - 1)
    owners = place_owner(owners, MEMBERS // 2, 0)
    offsets = jax.random.randint(second_key, (MEMBERS,), 0, FR_DEV)
    return (owners * FR_DEV + offsets).astype(jnp.int32)


def draw_legendre(key, part):
    key = jax.random.fold_in(key, 11)
    values = jax.random.truncated_normal(key, -6.0, 6.0, (MW, LAT, L), jnp.float32) * LAT ** (-0.5)
    orders = jnp.arange(MW, dtype=jnp.int32)[:, None, None]
    totals = jnp.arange(L, dtype=jnp.int32)[None, None, :]
    kept = (totals >= orders).astype(jnp.float32)
    return (values * kept).astype(jnp.bfloat16)


def levels(key, extent, cuts, least, top_value):
    level = 1.0
    for dim, blocks in cuts:
        draws = jax.random.uniform(jax.random.fold_in(jax.random.fold_in(key, 6), dim), (blocks,), jnp.float32, least / len(cuts), top_value / len(cuts))
        level = level * jnp.repeat(jnp.exp(draws), extent[dim] // blocks).reshape((-1,) + (1,) * (len(extent) - 1 - dim))
    return level


def normal_values(own_key, dims, scale, most, shards=(), held_as=jnp.bfloat16):
    values = scale * jax.random.normal(own_key, dims, jnp.float32)
    if shards:
        values = values * levels(own_key, dims, shards, -0.22, 0.18)
    return jnp.clip(values, -most, most).astype(held_as)


def setup_inputs(seed: int = 0) -> dict:
    streams_of = jax.random.split(jax.random.key(seed), 8)
    return {
        "frames": normal_values(streams_of[0], (FRAMES, LAT, LON, CH), 1.0, 6.0, ((0, 8), (1, 32))),
        "window": draw_window(jax.random.fold_in(streams_of[7], 71), 0),
        "targets": normal_values(streams_of[2], (MEMBERS, LAT, LON, CH), 0.25, 1.5, ((0, 8), (1, 32))),
        "w_in": normal_values(streams_of[3], (MEMBERS, CH, HID), CH ** -0.5, 0.5, ((0, 8),)),
        "w_out": normal_values(streams_of[4], (MEMBERS, HID, CH), HID ** -0.5, 0.375, ((0, 8),)),
        "legendre": draw_legendre(jax.random.fold_in(streams_of[7], 71), 0),
        "damping": jnp.clip(jnp.exp(jax.random.uniform(streams_of[6], (L,), jnp.float32, math.log(0.2), math.log(0.6))), 0.2, 0.6),
    }


relaxation = 1.0

def fourier_matrix(longitudes, orders):
    points = jnp.arange(longitudes, dtype=jnp.int32)[:, None]
    angles = 2.0 * math.pi / longitudes * (points * orders[None, :] % longitudes).astype(jnp.float32)
    factor = math.sqrt(2.0 / longitudes)
    paired = jnp.stack([factor * jnp.cos(angles), -factor * jnp.sin(angles)], axis=2)
    return paired.reshape(longitudes, 2 * orders.shape[0]).astype(jnp.bfloat16)

def lowered(values):
    return lax.optimization_barrier(values.astype(jnp.bfloat16))

def across(left, right):
    return lax.dot_general(left, right, (((0,), (0,)), ((), ())), preferred_element_type=jnp.float32)

def against(left, right):
    return lax.dot_general(left, right, (((1,), (1,)), ((), ())), preferred_element_type=jnp.float32)

def spectral(field_low, fourier, legendre, damping):
    wide = fourier.astype(jnp.float32)
    spectra = lowered(jnp.einsum('anc,nj->ajc', field_low.astype(jnp.float32), wide))
    halves = spectra.reshape(LAT, MW, 2, CH).astype(jnp.float32)
    coefficients = jnp.einsum('mal,amrc->mlrc', legendre.astype(jnp.float32), halves)
    coefficients = lowered(coefficients * damping[None, :, None, None])
    returned = lowered(jnp.einsum('mal,mlrc->amrc', legendre.astype(jnp.float32), coefficients.astype(jnp.float32)))
    returned = returned.reshape(LAT, 2 * MW, CH).astype(jnp.float32)
    return jnp.einsum('ajc,nj->anc', returned, wide)

def member_gradients(first_frame, target, w_in, w_out, fourier, legendre, damping):
    current = first_frame.astype(jnp.float32)
    history = []
    for section_index in range(STEPS):
        lowered_cells = lowered(current).reshape(-1, CH)
        hidden = lowered(jnp.tanh(jnp.dot(lowered_cells, w_in, preferred_element_type=jnp.float32)))
        moved = current + jnp.dot(hidden, w_out, preferred_element_type=jnp.float32).reshape(current.shape)
        current = moved - relaxation * spectral(lowered(moved), fourier, legendre, damping)
        history.append((lowered_cells, hidden))
    adjoint = (current - target.astype(jnp.float32)) / LAT
    sum_in = jnp.zeros((CH, HID), jnp.float32)
    sum_out = jnp.zeros((HID, CH), jnp.float32)
    for section_index in reversed(range(STEPS)):
        lowered_cells, hidden = history[section_index]
        pulled = adjoint - relaxation * spectral(lowered(adjoint), fourier, legendre, damping)
        pulled_low = lowered(pulled).reshape(-1, CH)
        sum_out = sum_out + across(hidden, pulled_low)
        hidden_wide = hidden.astype(jnp.float32)
        inner = lowered(against(pulled_low, w_out) * (1.0 - hidden_wide * hidden_wide))
        sum_in = sum_in + across(lowered_cells, inner)
        if section_index > 0:
            adjoint = pulled + against(inner, w_in).reshape(pulled.shape)
    return (sum_in, sum_out)

def reference(frames, window, targets, w_in, w_out, legendre, damping):
    fourier = fourier_matrix(LON, jnp.arange(MW, dtype=jnp.int32))

    def one_member(member_index):
        first_frame = lax.dynamic_index_in_dim(frames, window[member_index], 0, keepdims=False)
        target = lax.dynamic_index_in_dim(targets, member_index, 0, keepdims=False)
        first_layer = lax.dynamic_index_in_dim(w_in, member_index, 0, keepdims=False)
        second_layer = lax.dynamic_index_in_dim(w_out, member_index, 0, keepdims=False)
        return member_gradients(first_frame, target, first_layer, second_layer, fourier, legendre, damping)
    gathered = lax.map(one_member, jnp.arange(MEMBERS, dtype=jnp.int32))
    return (gathered[0], gathered[1])
```

```python
import math

import jax
import jax.numpy as jnp
import numpy as np
from jax import lax
from jax.sharding import Mesh, PartitionSpec as P

LAT = 256
STEPS = 3

EVERY = ("x", "z", "y", "core")
PLANE = ("x", "y", "core")
MEMBER = ("y", "core")


def fourier_matrix(longitudes, orders):
    points = np.arange(longitudes, dtype=np.int32)[:, None]
    angles = (2.0 * math.pi / longitudes * (points * orders[None, :] % longitudes)).astype(
        np.float32
    )
    factor = math.sqrt(2.0 / longitudes)
    paired = np.stack([factor * np.cos(angles), -factor * np.sin(angles)], axis=2)
    return paired.astype(np.float32).reshape(longitudes, 2 * orders.shape[0])


def across(left, right):
    return lax.dot_general(
        left, right, (((0,), (0,)), ((), ())), preferred_element_type=jnp.float32
    )


def against(left, right):
    return lax.dot_general(
        left, right, (((1,), (1,)), ((), ())), preferred_element_type=jnp.float32
    )


def exchange(values, axes):
    return lax.all_to_all(values, axes, split_axis=0, concat_axis=0, tiled=True)


def to_modes(field_low, fourier):
    return jnp.einsum(
        "anc,nj->jac", field_low, fourier, preferred_element_type=jnp.float32
    ).astype(jnp.bfloat16)


def to_grid(gridded, fourier):
    return jnp.einsum("jac,nj->anc", gridded, fourier, preferred_element_type=jnp.float32)


def filtered(spectra, legendre, damping):
    coefficients = jnp.einsum(
        "moal,omrac->mlrc", legendre, spectra, preferred_element_type=jnp.float32
    )
    coefficients = (coefficients * damping[None, :, None, None]).astype(jnp.bfloat16)
    return jnp.einsum(
        "moal,mlrc->omrac", legendre, coefficients, preferred_element_type=jnp.float32
    )


def body(frames, window, targets, w_in, w_out, legendre, damping):
    rows, longitudes, channels = frames.shape[1:]
    hidden_units = w_in.shape[2]
    size_x, size_z = lax.axis_size("x"), lax.axis_size("z")
    members = lax.axis_size(MEMBER)
    owners = size_x * members
    modes_local = legendre.shape[0]
    width = 2 * modes_local
    place = lax.axis_index(MEMBER)
    plane = lax.axis_index("z")

    layers = jnp.concatenate([w_in[0].reshape(-1, 128), w_out[0].reshape(-1, 128)], axis=0)
    layers = lax.all_gather(layers, MEMBER)
    layers = lax.dynamic_index_in_dim(layers, plane, 0, keepdims=False)
    half = layers.shape[0] // 2
    first_layer = layers[:half].reshape(w_in.shape[1:])
    second_layer = layers[half:].reshape(w_out.shape[1:])

    table = lax.dynamic_index_in_dim(legendre, place, 0, keepdims=False)
    table = lax.all_gather(table, "z")
    table = table.reshape(modes_local, size_x, size_z, rows, table.shape[2])
    table = table.transpose(0, 1, 3, 2, 4).reshape(modes_local, owners, rows, -1)

    both = exchange(jnp.stack([frames[0], targets[0]], axis=1), MEMBER)
    frame = exchange(jnp.take(both[:, 0], window, axis=0), "z")
    held, frame = lax.optimization_barrier((both[:, 1], frame))
    held = lax.all_gather(held, "z")
    target = lax.dynamic_index_in_dim(held, plane, 1, keepdims=False)

    ordered = np.arange(modes_local * owners, dtype=np.int32)
    ordered = ordered.reshape(size_x, size_z, members).transpose(0, 2, 1).reshape(-1)
    fourier = jnp.asarray(fourier_matrix(longitudes, ordered)).astype(jnp.bfloat16)

    mode = (lax.axis_index("x") * size_z + jnp.arange(modes_local)) * members + place
    norms = jnp.where(mode[:, None] == 0, jnp.array([[2.0, 0.0]]), 1.0)

    def unfold(values):
        return values.reshape(owners, modes_local, 2, rows, channels)

    current = frame.astype(jnp.float32)
    history = []
    for step in range(STEPS):
        lowered_cells = current.astype(jnp.bfloat16).reshape(-1, channels)
        hidden = jnp.tanh(
            jnp.dot(lowered_cells, first_layer, preferred_element_type=jnp.float32)
        ).astype(jnp.bfloat16)
        moved = current + jnp.dot(hidden, second_layer, preferred_element_type=jnp.float32).reshape(
            current.shape
        )
        history.append((lowered_cells, hidden))
        spectra = to_modes(moved.astype(jnp.bfloat16), fourier)
        if step < STEPS - 1:
            received = unfold(exchange(spectra, PLANE))
            returned = filtered(received, table, damping).astype(jnp.bfloat16)
            gridded = exchange(returned.reshape(-1, rows, channels), PLANE)
            current = moved - to_grid(gridded, fourier)
    spectra = jnp.stack(
        [
            spectra.reshape(owners, width, rows, channels),
            to_modes(target, fourier).reshape(owners, width, rows, channels),
        ],
        axis=1,
    )
    received = exchange(spectra, PLANE)
    ahead, aim = unfold(received[:, 0]), unfold(received[:, 1])
    first = filtered(ahead, table, damping)
    second = (
        2.0 * ahead.astype(jnp.float32)
        - aim.astype(jnp.float32)
        - norms[None, :, :, None, None] * first
    ).astype(jnp.bfloat16)
    returned = filtered(second, table, damping).astype(jnp.bfloat16)
    gridded = exchange(returned.reshape(-1, rows, channels), PLANE)
    pulled = (moved - target.astype(jnp.float32) - to_grid(gridded, fourier)) / LAT

    sum_in = jnp.zeros(first_layer.shape, jnp.float32)
    sum_out = jnp.zeros(second_layer.shape, jnp.float32)
    for step in reversed(range(STEPS)):
        lowered_cells, hidden = history[step]
        if step < STEPS - 1:
            received = unfold(exchange(to_modes(adjoint.astype(jnp.bfloat16), fourier), PLANE))
            returned = filtered(received, table, damping).astype(jnp.bfloat16)
            gridded = exchange(returned.reshape(-1, rows, channels), PLANE)
            pulled = adjoint - to_grid(gridded, fourier)
        pulled_low = pulled.astype(jnp.bfloat16).reshape(-1, channels)
        sum_out = sum_out + across(hidden, pulled_low)
        hidden_wide = hidden.astype(jnp.float32)
        inner = (against(pulled_low, second_layer) * (1.0 - hidden_wide * hidden_wide)).astype(
            jnp.bfloat16
        )
        sum_in = sum_in + across(lowered_cells, inner)
        if step > 0:
            adjoint = pulled + against(inner, first_layer).reshape(pulled.shape)

    sums = jnp.concatenate([sum_in.reshape(-1, 128), sum_out.reshape(-1, 128)], axis=0)
    height = sums.shape[0] // owners
    pieces = exchange(sums, PLANE).reshape(owners, height, 128).sum(axis=0)
    around = exchange(jnp.broadcast_to(pieces[None], (size_z, height, 128)), "z")
    spread = jnp.broadcast_to(around[None], (size_x, members, height, 128))
    total = exchange(spread.reshape(-1, 128), PLANE)
    half = total.shape[0] // 2
    return (
        total[:half].reshape((1,) + first_layer.shape),
        total[half:].reshape((1,) + second_layer.shape),
    )


def solution(mesh):
    fine = Mesh(mesh.devices.reshape(4, 8, 4, 2), EVERY)
    lat, member = ("x", "z"), MEMBER
    return jax.shard_map(
        body,
        mesh=fine,
        in_specs=(
            P(member, lat, None, None),
            P(),
            P(member, lat, None, None),
            P(member, None, None),
            P(member, None, None),
            P(lat, None, None),
            P(),
        ),
        out_specs=(P(member, None, None), P(member, None, None)),
        check_vma=False,
    )
```

```python
import functools
import math

import jax
import jax.numpy as jnp
import numpy as np
from jax import lax
from jax.experimental import pallas as pl
from jax.experimental.pallas import tpu as pltpu
from jax.sharding import Mesh, PartitionSpec as P

LAT = 256
STEPS = 3

EVERY = ("x", "z", "y", "core")
PLANE = ("x", "y", "core")
MEMBER = ("y", "core")

PAIR = 2
SHARE = 4
VMEM = 24 * 1024 * 1024
COPY_VMEM = 58 * 1024 * 1024


def fourier_matrix(longitudes, orders):
    points = np.arange(longitudes, dtype=np.int32)[:, None]
    angles = (2.0 * math.pi / longitudes * (points * orders[None, :] % longitudes)).astype(
        np.float32
    )
    factor = math.sqrt(2.0 / longitudes)
    paired = np.stack([factor * np.cos(angles), -factor * np.sin(angles)], axis=2)
    return paired.astype(np.float32).reshape(longitudes, 2 * orders.shape[0])


def across(left, right):
    return lax.dot_general(
        left, right, (((0,), (0,)), ((), ())), preferred_element_type=jnp.float32
    )


def exchange(values, axes):
    return lax.all_to_all(values, axes, split_axis=0, concat_axis=0, tiled=True)


def dot(left, right):
    return jnp.dot(left, right, preferred_element_type=jnp.float32)


def row_of(wide, row, rows):
    return wide[pl.ds(row, wide.shape[0] // rows, stride=rows), :]


def side_by_side(parts):
    return jnp.concatenate(parts, axis=1)


def to_grid(wide, fourier, first, rows):
    lines = [row_of(wide, first + i, rows).astype(jnp.bfloat16) for i in range(PAIR)]
    grid = dot(fourier[...], side_by_side(lines))
    return [grid[:, i * 128 : (i + 1) * 128] for i in range(PAIR)]


def to_modes(wide, turned, fields, first, rows):
    spectra = dot(turned[...], side_by_side(fields))
    for i in range(PAIR):
        wide[pl.ds(first + i, spectra.shape[0], stride=rows), :] = spectra[
            :, i * 128 : (i + 1) * 128
        ]


def network(current, w_in, w_out, low_ref, hidden_ref, i):
    low = current.astype(jnp.bfloat16)
    hidden = jnp.tanh(dot(low, w_in[...])).astype(jnp.bfloat16)
    low_ref[i] = low
    hidden_ref[i] = hidden
    return current + dot(hidden, w_out[...])


def by_pairs(rows):
    def wrapped(run):
        lax.fori_loop(0, rows // PAIR, lambda g, carry: (run(g * PAIR), carry)[1], 0, unroll=2)

    return wrapped


def start_kernel(rows, frame, turned, w_in, w_out, spectra, moved, low, hidden, wide):
    @by_pairs(rows)
    def _(first):
        fields = []
        for i in range(PAIR):
            current = frame[first + i].astype(jnp.float32)
            value = network(current, w_in, w_out, low, hidden, first + i)
            moved[first + i] = value
            fields.append(value.astype(jnp.bfloat16))
        to_modes(wide, turned, fields, first, rows)

    spectra[...] = wide[...].astype(jnp.bfloat16)


def ahead_kernel(rows, last, returned, before, fourier, turned, w_in, w_out, *rest):
    if last:
        aim, spectra, moved, low, hidden, back, wide = rest
    else:
        spectra, moved, low, hidden, back, wide = rest
    back[...] = returned[...].astype(jnp.float32)

    @by_pairs(rows)
    def _(first):
        grid = to_grid(back, fourier, first, rows)
        fields = []
        for i in range(PAIR):
            value = network(before[first + i] - grid[i], w_in, w_out, low, hidden, first + i)
            moved[first + i] = value
            fields.append(value.astype(jnp.bfloat16))
        to_modes(wide, turned, fields, first, rows)

    lines = wide[...].astype(jnp.bfloat16)
    if last:
        spectra[:, 0] = lines.reshape(spectra.shape[0], -1, 128)
        spectra[:, 1] = aim[...].reshape(spectra.shape[0], -1, 128)
    else:
        spectra[...] = lines


def aim_kernel(rows, target, turned, spectra, wide):
    @by_pairs(rows)
    def _(first):
        to_modes(wide, turned, [target[first + i] for i in range(PAIR)], first, rows)

    spectra[...] = wide[...].astype(jnp.bfloat16)


def adjoint_kernel(rows, first_one, last, returned, base, *rest):
    rest = list(rest)
    target = rest.pop(0) if first_one else None
    hidden, fourier, out_t = rest[:3]
    rest = rest[3:]
    if last:
        low, inner_ref, back = rest
    else:
        turned, in_t, spectra, adjoint, low, inner_ref, back, wide = rest
    back[...] = returned[...].astype(jnp.float32)

    @by_pairs(rows)
    def _(first):
        grid = to_grid(back, fourier, first, rows)
        fields = []
        for i in range(PAIR):
            row = first + i
            if first_one:
                pulled = (base[row] - target[row].astype(jnp.float32) - grid[i]) * (1.0 / LAT)
            else:
                pulled = base[row] - grid[i]
            pulled_low = pulled.astype(jnp.bfloat16)
            low[row] = pulled_low
            wide_hidden = hidden[row].astype(jnp.float32)
            inner = (dot(pulled_low, out_t[...]) * (1.0 - wide_hidden * wide_hidden)).astype(
                jnp.bfloat16
            )
            inner_ref[row] = inner
            if not last:
                value = pulled + dot(inner, in_t[...])
                adjoint[row] = value
                fields.append(value.astype(jnp.bfloat16))
        if not last:
            to_modes(wide, turned, fields, first, rows)

    if not last:
        spectra[...] = wide[...].astype(jnp.bfloat16)


def gather_lines(block, k):
    values = block[:, k].astype(jnp.float32)
    owners, pair, channels = values.shape
    values = values.reshape(owners, 2, pair // 2, channels)
    return side_by_side([values[:, r].reshape(-1, channels) for r in range(2)])


def scatter_lines(out, k, values):
    owners = out.shape[0]
    halves = [values[:, r * 128 : (r + 1) * 128].reshape(owners, 1, -1, 128) for r in range(2)]
    lines = jnp.concatenate(halves, axis=1)
    out[:, k] = lines.reshape(owners, -1, 128).astype(jnp.bfloat16)


def filtered(spectra, table, turned, damping):
    coefficients = (dot(turned, spectra) * damping[...]).astype(jnp.bfloat16)
    return dot(table, coefficients)


def filter_kernel(received, table, turned, damping, out):
    @pl.loop(0, table.shape[0], step=SHARE)
    def _(first):
        for k in [first + i for i in range(SHARE)]:
            spectra = gather_lines(received, k).astype(jnp.bfloat16)
            scatter_lines(out, k, filtered(spectra, table[k], turned[k], damping))


def filter_twice_kernel(received, norms, table, turned, damping, out):
    @pl.loop(0, table.shape[0], step=SHARE)
    def _(start):
        for k in [start + i for i in range(SHARE)]:
            spectra = gather_lines(received.at[:, 0], k)
            first = filtered(spectra.astype(jnp.bfloat16), table[k], turned[k], damping)
            second = 2.0 * spectra - gather_lines(received.at[:, 1], k) - norms[k] * first
            scatter_lines(
                out, k, filtered(second.astype(jnp.bfloat16), table[k], turned[k], damping)
            )


def params():
    return pltpu.CompilerParams(vmem_limit_bytes=VMEM)


def shaped(shape, dtype):
    return jax.ShapeDtypeStruct(shape, dtype)


def through(copies, slots, in_sems, out_sems):
    ins = [
        pltpu.make_async_copy(a, slots.at[i], in_sems.at[i]) for i, (a, _) in enumerate(copies)
    ]
    outs = [
        pltpu.make_async_copy(slots.at[i], b, out_sems.at[i]) for i, (_, b) in enumerate(copies)
    ]
    for copy in ins:
        copy.start()
    for copy, after in zip(ins, outs):
        copy.wait()
        after.start()
    for copy in outs:
        copy.wait()


def by_copies(kernel, out_shape, count, block, dtype, name, *operands, window=None):
    anywhere = pl.BlockSpec(memory_space=pl.ANY)
    in_specs = [anywhere] * len(operands)
    if window is not None:
        operands = (window,) + operands
        in_specs = [pl.BlockSpec(memory_space=pltpu.SMEM)] + in_specs
    return pl.pallas_call(
        kernel,
        in_specs=in_specs,
        out_specs=jax.tree.map(lambda _: anywhere, out_shape),
        out_shape=out_shape,
        scratch_shapes=[
            pltpu.VMEM((count,) + block, dtype),
            pltpu.SemaphoreType.DMA((count,)),
            pltpu.SemaphoreType.DMA((count,)),
        ],
        compiler_params=pltpu.CompilerParams(vmem_limit_bytes=COPY_VMEM),
        name=name,
    )(*operands)


def paired_kernel(first, second, out, *scratch):
    rows = first.shape[0]
    through(
        [(first.at[s], out.at[s, 0]) for s in range(rows)]
        + [(second.at[s], out.at[s, 1]) for s in range(rows)],
        *scratch,
    )


def paired(first, second):
    rows = first.shape[0]
    block = first.shape[1:]
    out = shaped((rows, 2) + block, first.dtype)
    return by_copies(paired_kernel, out, 2 * rows, block, first.dtype, "paired", first, second)


def chosen_kernel(window, both, frame, held, *scratch):
    members = frame.shape[0]
    through(
        [(both.at[window[k], 0], frame.at[k]) for k in range(members)]
        + [(both.at[k, 1], held.at[k]) for k in range(members)],
        *scratch,
    )


def chosen(window, both):
    members = both.shape[0]
    block = both.shape[2:]
    out = [shaped((members,) + block, both.dtype)] * 2
    window = jnp.clip(window, 0, members - 1)
    return by_copies(
        chosen_kernel, out, 2 * members, block, both.dtype, "chosen", both, window=window
    )


def body(frames, window, targets, w_in, w_out, legendre, damping):
    rows, longitudes, channels = frames.shape[1:]
    units = w_in.shape[2]
    size_x, size_z = lax.axis_size("x"), lax.axis_size("z")
    members = lax.axis_size(MEMBER)
    owners = size_x * members
    modes = legendre.shape[0]
    degrees = legendre.shape[2]
    lines = owners * 2 * modes * rows
    width = 2 * modes * owners
    place = lax.axis_index(MEMBER)
    plane = lax.axis_index("z")
    bf16, f32 = jnp.bfloat16, jnp.float32

    swap = [
        ((x * size_z + z) * members + k, (x * size_z + k) * members + z)
        for x in range(size_x)
        for z in range(size_z)
        for k in range(members)
    ]
    first_layer = lax.ppermute(w_in[0], EVERY, swap)
    second_layer = lax.ppermute(w_out[0], EVERY, swap)

    table = lax.dynamic_index_in_dim(legendre, place, 0, keepdims=False)
    table, window = lax.optimization_barrier((table, window))
    table = lax.all_gather(table, "z")

    both = exchange(paired(frames[0], targets[0]), MEMBER)
    both, table, first_layer, second_layer = lax.optimization_barrier(
        (both, table, first_layer, second_layer)
    )
    frame, held = chosen(window, both)
    frame = exchange(frame, "z")
    held, frame = lax.optimization_barrier((held, frame))
    held = lax.all_gather(held, "z")

    table = table.reshape(modes, size_x, size_z, rows, degrees)
    table = table.transpose(0, 1, 3, 2, 4).reshape(modes, owners * rows, degrees)
    turned_table = table.transpose(0, 2, 1)

    ordered = np.arange(modes * owners, dtype=np.int32)
    ordered = ordered.reshape(size_x, size_z, members).transpose(0, 2, 1).reshape(-1)
    matrix = fourier_matrix(longitudes, ordered)
    fourier = jnp.asarray(matrix).astype(bf16)
    turned = jnp.asarray(np.ascontiguousarray(matrix.T)).astype(bf16)

    mode = (lax.axis_index("x") * size_z + jnp.arange(modes)) * members + place
    norms = jnp.where(mode[:, None] == 0, jnp.array([[2.0, 0.0]]), 1.0)
    norms = jnp.repeat(norms, channels, axis=1).reshape(modes, 1, 2 * channels)
    decay = jnp.broadcast_to(damping[:, None], (degrees, 2 * channels))

    shape = (rows, longitudes, channels)
    deep_shape = (rows, longitudes, units)
    buffer = pltpu.VMEM((lines, channels), f32)

    def forward(returned, before, aim=None):
        last = aim is not None
        if returned is None:
            kernel = functools.partial(start_kernel, rows)
            operands = [before, turned, first_layer, second_layer]
            scratch = [buffer]
        else:
            kernel = functools.partial(ahead_kernel, rows, last)
            operands = [returned, before, fourier, turned, first_layer, second_layer]
            scratch = [buffer, buffer]
            if last:
                operands.append(aim)
        if last:
            out_shape = (owners, 2, lines // owners, channels)
        else:
            out_shape = (lines, channels)
        cells = rows * longitudes
        return pl.pallas_call(
            kernel,
            out_shape=[
                shaped(out_shape, bf16),
                shaped(shape, f32),
                shaped(shape, bf16),
                shaped(deep_shape, bf16),
            ],
            scratch_shapes=scratch,
            compiler_params=params(),
            cost_estimate=pl.CostEstimate(
                flops=4 * cells * channels * (units + width),
                bytes_accessed=9 * cells * channels * 2,
                transcendentals=cells * units,
            ),
            name="forward",
        )(*operands)

    def transformed(target):
        return pl.pallas_call(
            functools.partial(aim_kernel, rows),
            out_shape=shaped((lines, channels), bf16),
            scratch_shapes=[buffer],
            compiler_params=params(),
            cost_estimate=pl.CostEstimate(
                flops=2 * rows * longitudes * channels * width,
                bytes_accessed=4 * lines * channels,
                transcendentals=0,
            ),
            name="aim",
        )(target, turned)

    def adjoint_of(returned, base, hidden, target=None, last=False):
        first = target is not None
        operands = [returned, base] + ([target] if first else []) + [hidden, fourier, out_t]
        outs = [shaped(shape, bf16), shaped(deep_shape, bf16)]
        scratch = [buffer]
        if not last:
            operands += [turned, in_t]
            outs = [shaped((lines, channels), bf16), shaped(shape, f32)] + outs
            scratch = [buffer, buffer]
        cells = rows * longitudes
        return pl.pallas_call(
            functools.partial(adjoint_kernel, rows, first, last),
            out_shape=outs,
            scratch_shapes=scratch,
            compiler_params=params(),
            cost_estimate=pl.CostEstimate(
                flops=4 * cells * channels * (units + width),
                bytes_accessed=11 * cells * channels * 2,
                transcendentals=0,
            ),
            name="adjoint",
        )(*operands)

    blocks = (owners, modes, 2 * rows, channels)

    def filtering(received):
        out = pl.pallas_call(
            filter_kernel,
            out_shape=shaped(blocks, bf16),
            compiler_params=params(),
            cost_estimate=pl.CostEstimate(
                flops=8 * lines * channels * degrees,
                bytes_accessed=8 * lines * channels,
                transcendentals=0,
            ),
            name="filter",
        )(received.reshape(blocks), table, turned_table, decay)
        return out.reshape(lines, channels)

    def filtering_twice(received):
        received = received.reshape(owners, 2, modes, 2 * rows, channels)
        out = pl.pallas_call(
            filter_twice_kernel,
            out_shape=shaped(blocks, bf16),
            compiler_params=params(),
            cost_estimate=pl.CostEstimate(
                flops=16 * lines * channels * degrees,
                bytes_accessed=10 * lines * channels,
                transcendentals=0,
            ),
            name="filter_twice",
        )(received, norms, table, turned_table, decay)
        return out.reshape(lines, channels)

    in_t, out_t = first_layer.T, second_layer.T
    table, turned_table, decay, norms, in_t, out_t, first_layer, second_layer, frame = (
        lax.optimization_barrier(
            (table, turned_table, decay, norms, in_t, out_t, first_layer, second_layer, frame)
        )
    )
    history = []
    moved, returned, aim = frame, None, None
    for step in range(STEPS):
        if step == STEPS - 1:
            held, returned = lax.optimization_barrier((held, returned))
            target = lax.dynamic_index_in_dim(held, plane, 1, keepdims=False)
            aim = transformed(target)
        spectra, moved, low, hidden = forward(returned, moved, aim)
        history.append((low, hidden))
        if step < STEPS - 1:
            returned = exchange(filtering(exchange(spectra, PLANE)), PLANE)
    received = exchange(spectra, PLANE)
    returned = exchange(filtering_twice(received), PLANE)

    sum_in = jnp.zeros(first_layer.shape, f32)
    sum_out = jnp.zeros(second_layer.shape, f32)
    adjoint = moved
    for step in reversed(range(STEPS)):
        low, hidden = history[step]
        if step > 0:
            spectra, adjoint, pulled, inner = adjoint_of(
                returned, adjoint, hidden, target if step == STEPS - 1 else None
            )
        else:
            pulled, inner = adjoint_of(returned, adjoint, hidden, None, True)
        sum_out = sum_out + across(hidden.reshape(-1, units), pulled.reshape(-1, channels))
        sum_in = sum_in + across(low.reshape(-1, channels), inner.reshape(-1, units))
        if step > 0:
            sum_in, sum_out, spectra = lax.optimization_barrier((sum_in, sum_out, spectra))
            returned = exchange(filtering(exchange(spectra, PLANE)), PLANE)

    sums = jnp.concatenate([sum_in.reshape(-1, 128), sum_out.reshape(-1, 128)], axis=0)
    height = sums.shape[0] // owners
    pieces = exchange(sums, PLANE).reshape(owners, height, 128).sum(axis=0)
    around = exchange(jnp.broadcast_to(pieces[None], (size_z, height, 128)), "z")
    spread = jnp.broadcast_to(around[None], (size_x, members, height, 128))
    total = exchange(spread.reshape(-1, 128), PLANE)
    half = total.shape[0] // 2
    return (
        total[:half].reshape((1,) + first_layer.shape),
        total[half:].reshape((1,) + second_layer.shape),
    )


def solution(mesh):
    fine = Mesh(mesh.devices.reshape(4, 8, 4, 2), EVERY)
    lat, member = ("x", "z"), MEMBER
    return jax.shard_map(
        body,
        mesh=fine,
        in_specs=(
            P(member, lat, None, None),
            P(),
            P(member, lat, None, None),
            P(member, None, None),
            P(member, None, None),
            P(lat, None, None),
            P(),
        ),
        out_specs=(P(member, None, None), P(member, None, None)),
        check_vma=False,
    )
```

```python
import functools
import math

import jax
import jax.numpy as jnp
import numpy as np
from jax import lax
from jax.experimental import pallas as pl
from jax.experimental.pallas import tpu as pltpu
from jax.sharding import Mesh, PartitionSpec as P

LAT = 256
STEPS = 3

EVERY = ("x", "z", "y", "core")
PLANE = ("x", "y", "core")
MEMBER = ("y", "core")

PAIR = 2
SHARE = 4
VMEM = 24 * 1024 * 1024
MOST = 58 * 1024 * 1024


def fourier_matrix(longitudes, orders):
    points = np.arange(longitudes, dtype=np.int32)[:, None]
    angles = (2.0 * math.pi / longitudes * (points * orders[None, :] % longitudes)).astype(
        np.float32
    )
    factor = math.sqrt(2.0 / longitudes)
    paired = np.stack([factor * np.cos(angles), -factor * np.sin(angles)], axis=2)
    return paired.astype(np.float32).reshape(longitudes, 2 * orders.shape[0])


def across(left, right):
    return lax.dot_general(
        left, right, (((0,), (0,)), ((), ())), preferred_element_type=jnp.float32
    )


def exchange(values, axes):
    return lax.all_to_all(values, axes, split_axis=0, concat_axis=0, tiled=True)


def dot(left, right):
    return jnp.dot(left, right, preferred_element_type=jnp.float32)


def row_of(wide, row, rows):
    return wide[pl.ds(row, wide.shape[0] // rows, stride=rows), :]


def side_by_side(parts):
    return jnp.concatenate(parts, axis=1)


def to_grid(wide, fourier, first, rows):
    lines = [row_of(wide, first + i, rows).astype(jnp.bfloat16) for i in range(PAIR)]
    grid = dot(fourier[...], side_by_side(lines))
    return [grid[:, i * 128 : (i + 1) * 128] for i in range(PAIR)]


def to_modes(wide, turned, fields, first, rows):
    spectra = dot(turned[...], side_by_side(fields))
    for i in range(PAIR):
        wide[pl.ds(first + i, spectra.shape[0], stride=rows), :] = spectra[
            :, i * 128 : (i + 1) * 128
        ]


def network(current, w_in, w_out, low_ref, hidden_ref, moved_ref, row):
    low = current.astype(jnp.bfloat16)
    hidden = jnp.tanh(dot(low, w_in[...])).astype(jnp.bfloat16)
    moved = current + dot(hidden, w_out[...])
    low_ref[row] = low
    hidden_ref[row] = hidden
    moved_ref[row] = moved
    return moved.astype(jnp.bfloat16)


def by_pairs(rows):
    def wrapped(run):
        for first in range(0, rows, PAIR):
            run(first)

    return wrapped


def start_kernel(rows, frame, turned, w_in, w_out, spectra, moved, low, hidden, wide):
    @by_pairs(rows)
    def _(first):
        fields = [
            network(frame[row].astype(jnp.float32), w_in, w_out, low, hidden, moved, row)
            for row in range(first, first + PAIR)
        ]
        to_modes(wide, turned, fields, first, rows)

    spectra[...] = wide[...].astype(jnp.bfloat16)


def ahead_kernel(rows, last, returned, before, fourier, turned, w_in, w_out, *rest):
    if last:
        aim, spectra, moved, low, hidden, back, wide = rest
    else:
        spectra, moved, low, hidden, back, wide = rest
    back[...] = returned[...].astype(jnp.float32)

    @by_pairs(rows)
    def _(first):
        grid = to_grid(back, fourier, first, rows)
        fields = [
            network(before[first + i] - grid[i], w_in, w_out, low, hidden, moved, first + i)
            for i in range(PAIR)
        ]
        to_modes(wide, turned, fields, first, rows)

    if last:
        owners = spectra.shape[0]
        spectra[:, 0] = wide[...].astype(jnp.bfloat16).reshape(owners, -1, 128)
        spectra[:, 1] = aim[...].reshape(owners, -1, 128)
    else:
        spectra[...] = wide[...].astype(jnp.bfloat16)


def aim_kernel(rows, target, turned, spectra, wide):
    @by_pairs(rows)
    def _(first):
        to_modes(wide, turned, [target[first + i] for i in range(PAIR)], first, rows)

    spectra[...] = wide[...].astype(jnp.bfloat16)


def adjoint_kernel(rows, first_one, last, returned, base, *rest):
    rest = list(rest)
    target = rest.pop(0) if first_one else None
    low, hidden, fourier, out_t = rest[:4]
    rest = rest[4:]
    if last:
        sum_in, sum_out, sums, back, total_in, total_out = rest
    else:
        turned, in_t = rest[:2]
        rest = rest[2:]
        if first_one:
            sum_in = sum_out = None
        else:
            sum_in, sum_out = rest[:2]
            rest = rest[2:]
        spectra, adjoint, total_in, total_out, back, wide = rest
    back[...] = returned[...].astype(jnp.float32)
    if first_one:
        total_in[...] = jnp.zeros_like(total_in)
        total_out[...] = jnp.zeros_like(total_out)
    else:
        total_in[...] = sum_in[...]
        total_out[...] = sum_out[...]

    @by_pairs(rows)
    def _(first):
        grid = to_grid(back, fourier, first, rows)
        fields = []
        for i in range(PAIR):
            row = first + i
            if first_one:
                pulled = (base[row] - target[row].astype(jnp.float32) - grid[i]) * (1.0 / LAT)
            else:
                pulled = base[row] - grid[i]
            pulled_low = pulled.astype(jnp.bfloat16)
            units = hidden[row]
            total_out[...] += across(pulled_low, units)
            wide_units = units.astype(jnp.float32)
            inner = (dot(pulled_low, out_t[...]) * (1.0 - wide_units * wide_units)).astype(
                jnp.bfloat16
            )
            total_in[...] += across(low[row], inner)
            if not last:
                value = pulled + dot(inner, in_t[...])
                adjoint[row] = value
                fields.append(value.astype(jnp.bfloat16))
        if not last:
            to_modes(wide, turned, fields, first, rows)

    if last:
        height = total_in.shape[0]
        halves = total_in.shape[1] // 128
        for h in range(halves):
            part = slice(h * 128, (h + 1) * 128)
            sums[h * height : (h + 1) * height] = total_in[:, part]
            sums[(halves + h) * height : (halves + h + 1) * height] = total_out[:, part].T
    else:
        spectra[...] = wide[...].astype(jnp.bfloat16)


def parted_kernel(total, grad_in, grad_out):
    height = grad_in.shape[1]
    halves = grad_in.shape[2] // 128
    for h in range(halves):
        grad_in[0, :, h * 128 : (h + 1) * 128] = total[h * height : (h + 1) * height]
    grad_out[0] = total[halves * height :]


def gather_lines(block, k):
    values = block[:, k].astype(jnp.float32)
    owners, pair, channels = values.shape
    values = values.reshape(owners, 2, pair // 2, channels)
    return side_by_side([values[:, r].reshape(-1, channels) for r in range(2)])


def scatter_lines(out, k, values):
    owners = out.shape[0]
    halves = [values[:, r * 128 : (r + 1) * 128].reshape(owners, 1, -1, 128) for r in range(2)]
    lines = jnp.concatenate(halves, axis=1)
    out[:, k] = lines.reshape(owners, -1, 128).astype(jnp.bfloat16)


def filtered(spectra, table, turned, damping):
    coefficients = (dot(turned, spectra) * damping[...]).astype(jnp.bfloat16)
    return dot(table, coefficients)


def filter_kernel(received, table, turned, damping, out):
    @pl.loop(0, table.shape[0], step=SHARE)
    def _(first):
        for k in [first + i for i in range(SHARE)]:
            spectra = gather_lines(received, k).astype(jnp.bfloat16)
            scatter_lines(out, k, filtered(spectra, table[k], turned[k], damping))


def filter_twice_kernel(received, norms, table, turned, damping, out):
    @pl.loop(0, table.shape[0], step=SHARE)
    def _(start):
        for k in [start + i for i in range(SHARE)]:
            spectra = gather_lines(received.at[:, 0], k)
            first = filtered(spectra.astype(jnp.bfloat16), table[k], turned[k], damping)
            second = 2.0 * spectra - gather_lines(received.at[:, 1], k) - norms[k] * first
            scatter_lines(
                out, k, filtered(second.astype(jnp.bfloat16), table[k], turned[k], damping)
            )


def params(limit=VMEM):
    return pltpu.CompilerParams(vmem_limit_bytes=limit)


def shaped(shape, dtype):
    return jax.ShapeDtypeStruct(shape, dtype)


def in_smem():
    return pl.BlockSpec(memory_space=pltpu.SMEM)


def anywhere():
    return pl.BlockSpec(memory_space=pl.ANY)


def in_vmem():
    return pl.BlockSpec(memory_space=pltpu.VMEM)


def paired_kernel(first, second, out, slots, in_sems, out_sems):
    places = [(p, s) for p in range(2) for s in range(first.shape[0])]
    ins, outs = [], []
    for p, s in places:
        source = (first, second)[p].at[s]
        ins.append(pltpu.make_async_copy(source, slots.at[s, p], in_sems.at[p, s]))
        outs.append(pltpu.make_async_copy(slots.at[s, p], out.at[s, p], out_sems.at[p, s]))
    for copy in ins:
        copy.start()
    for copy, after in zip(ins, outs):
        copy.wait()
        after.start()
    for copy in outs:
        copy.wait()


def paired(first, second):
    rows = first.shape[0]
    shape = (rows, 2) + first.shape[1:]
    return pl.pallas_call(
        paired_kernel,
        in_specs=[anywhere()] * 2,
        out_specs=anywhere(),
        out_shape=shaped(shape, first.dtype),
        scratch_shapes=[
            pltpu.VMEM(shape, first.dtype),
            pltpu.SemaphoreType.DMA((2, rows)),
            pltpu.SemaphoreType.DMA((2, rows)),
        ],
        compiler_params=params(MOST),
        name="paired",
    )(first, second)


def chosen_kernel(window, both, frame, held):
    for k in range(frame.shape[0]):
        frame[k] = both[window[k], 0]
        held[k] = both[k, 1]


def chosen(window, both):
    members = both.shape[0]
    out = shaped((members,) + both.shape[2:], both.dtype)
    return pl.pallas_call(
        chosen_kernel,
        in_specs=[in_smem(), in_vmem()],
        out_specs=[in_vmem()] * 2,
        out_shape=[out, out],
        compiler_params=params(),
        name="chosen",
    )(jnp.clip(window, 0, members - 1), both)


def body(frames, window, targets, w_in, w_out, legendre, damping):
    rows, longitudes, channels = frames.shape[1:]
    units = w_in.shape[2]
    size_x, size_z = lax.axis_size("x"), lax.axis_size("z")
    members = lax.axis_size(MEMBER)
    owners = size_x * members
    modes = legendre.shape[0]
    degrees = legendre.shape[2]
    lines = owners * 2 * modes * rows
    width = 2 * modes * owners
    place = lax.axis_index(MEMBER)
    plane = lax.axis_index("z")
    bf16, f32 = jnp.bfloat16, jnp.float32

    swap = [
        ((x * size_z + z) * members + k, (x * size_z + k) * members + z)
        for x in range(size_x)
        for z in range(size_z)
        for k in range(members)
    ]
    first_layer = lax.ppermute(w_in[0], EVERY, swap)
    second_layer = lax.ppermute(w_out[0], EVERY, swap)

    table = lax.dynamic_index_in_dim(legendre, place, 0, keepdims=False)
    table = table.reshape(size_x, size_z, rows, degrees)
    table = table.transpose(0, 2, 1, 3).reshape(owners * rows, degrees)
    table, window = lax.optimization_barrier((table, window))
    table = lax.all_gather(table, "z")

    both = exchange(paired(frames[0], targets[0]), MEMBER)
    both, table, first_layer, second_layer = lax.optimization_barrier(
        (both, table, first_layer, second_layer)
    )
    frame, held = chosen(window, both)
    frame = exchange(frame, "z")
    held, frame = lax.optimization_barrier((held, frame))
    held = lax.all_gather(held, "z")

    table = table.reshape(modes, owners * rows, degrees)
    turned_table = table.transpose(0, 2, 1)

    ordered = np.arange(modes * owners, dtype=np.int32)
    ordered = ordered.reshape(size_x, size_z, members).transpose(0, 2, 1).reshape(-1)
    matrix = fourier_matrix(longitudes, ordered)
    fourier = jnp.asarray(matrix).astype(bf16)
    turned = jnp.asarray(np.ascontiguousarray(matrix.T)).astype(bf16)

    mode = (lax.axis_index("x") * size_z + jnp.arange(modes)) * members + place
    norms = jnp.where(mode[:, None] == 0, jnp.array([[2.0, 0.0]]), 1.0)
    norms = jnp.repeat(norms, channels, axis=1).reshape(modes, 1, 2 * channels)
    decay = jnp.broadcast_to(damping[:, None], (degrees, 2 * channels))

    shape = (rows, longitudes, channels)
    deep_shape = (rows, longitudes, units)
    buffer = pltpu.VMEM((lines, channels), f32)

    def forward(returned, before, aim=None):
        last = aim is not None
        if returned is None:
            kernel = functools.partial(start_kernel, rows)
            operands = [before, turned, first_layer, second_layer]
            scratch = [buffer]
        else:
            kernel = functools.partial(ahead_kernel, rows, last)
            operands = [returned, before, fourier, turned, first_layer, second_layer]
            operands += [aim] if last else []
            scratch = [buffer, buffer]
        cells = rows * longitudes
        return pl.pallas_call(
            kernel,
            out_shape=[
                shaped((owners, 2, lines // owners, channels) if last else (lines, channels), bf16),
                shaped(shape, f32),
                shaped(shape, bf16),
                shaped(deep_shape, bf16),
            ],
            scratch_shapes=scratch,
            compiler_params=params(),
            cost_estimate=pl.CostEstimate(
                flops=4 * cells * channels * (units + width),
                bytes_accessed=9 * cells * channels * 2,
                transcendentals=cells * units,
            ),
            name="forward",
        )(*operands)

    def transformed(target):
        return pl.pallas_call(
            functools.partial(aim_kernel, rows),
            out_shape=shaped((lines, channels), bf16),
            scratch_shapes=[buffer],
            compiler_params=params(),
            cost_estimate=pl.CostEstimate(
                flops=2 * rows * longitudes * channels * width,
                bytes_accessed=4 * lines * channels,
                transcendentals=0,
            ),
            name="aim",
        )(target, turned)

    def adjoint_of(returned, base, low, hidden, sums, target=None, last=False):
        first_one = target is not None
        operands = [returned, base] + ([target] if first_one else [])
        operands += [low, hidden, fourier, out_t]
        sum_shape = shaped(first_layer.shape, f32)
        accumulators = [pltpu.VMEM(first_layer.shape, f32)] * 2
        if last:
            operands += list(sums)
            outs = shaped((2 * units, channels), f32)
            scratch = [buffer] + accumulators
        else:
            operands += [turned, in_t] + ([] if first_one else list(sums))
            outs = [shaped((lines, channels), bf16), shaped(shape, f32), sum_shape, sum_shape]
            scratch = [buffer, buffer]
        cells = rows * longitudes
        return pl.pallas_call(
            functools.partial(adjoint_kernel, rows, first_one, last),
            out_shape=outs,
            scratch_shapes=scratch,
            compiler_params=params(),
            cost_estimate=pl.CostEstimate(
                flops=4 * cells * channels * (2 * units + width),
                bytes_accessed=11 * cells * channels * 2,
                transcendentals=0,
            ),
            name="adjoint",
        )(*operands)

    blocks = (owners, modes, 2 * rows, channels)

    def filtering(received):
        out = pl.pallas_call(
            filter_kernel,
            out_shape=shaped(blocks, bf16),
            compiler_params=params(),
            cost_estimate=pl.CostEstimate(
                flops=8 * lines * channels * degrees,
                bytes_accessed=8 * lines * channels,
                transcendentals=0,
            ),
            name="filter",
        )(received.reshape(blocks), table, turned_table, decay)
        return out.reshape(lines, channels)

    def filtering_twice(received):
        received = received.reshape(owners, 2, modes, 2 * rows, channels)
        out = pl.pallas_call(
            filter_twice_kernel,
            out_shape=shaped(blocks, bf16),
            compiler_params=params(),
            cost_estimate=pl.CostEstimate(
                flops=16 * lines * channels * degrees,
                bytes_accessed=10 * lines * channels,
                transcendentals=0,
            ),
            name="filter_twice",
        )(received, norms, table, turned_table, decay)
        return out.reshape(lines, channels)

    in_t, out_t = first_layer.T, second_layer.T
    table, turned_table, decay, norms, in_t, out_t, first_layer, second_layer, frame = (
        lax.optimization_barrier(
            (table, turned_table, decay, norms, in_t, out_t, first_layer, second_layer, frame)
        )
    )
    history = []
    moved, returned, aim = frame, None, None
    for step in range(STEPS):
        if step == STEPS - 1:
            held, returned = lax.optimization_barrier((held, returned))
            target = lax.dynamic_index_in_dim(held, plane, 1, keepdims=False)
            aim = transformed(target)
        spectra, moved, low, hidden = forward(returned, moved, aim)
        history.append((low, hidden))
        if step < STEPS - 1:
            returned = exchange(filtering(exchange(spectra, PLANE)), PLANE)
    received = exchange(spectra, PLANE)
    returned = exchange(filtering_twice(received), PLANE)

    sums = None
    adjoint = moved
    for step in reversed(range(1, STEPS)):
        low, hidden = history[step]
        spectra, adjoint, *sums = adjoint_of(
            returned, adjoint, low, hidden, sums, target if step == STEPS - 1 else None
        )
        returned = exchange(filtering(exchange(spectra, PLANE)), PLANE)
    low, hidden = history[0]
    sums = adjoint_of(returned, adjoint, low, hidden, sums, None, True)

    height = sums.shape[0] // owners
    pieces = exchange(sums, PLANE).reshape(owners, height, 128).sum(axis=0)
    around = exchange(jnp.broadcast_to(pieces[None], (size_z, height, 128)), "z")
    spread = jnp.broadcast_to(around[None], (size_x, members, height, 128))
    total = exchange(spread.reshape(-1, 128), PLANE)
    return tuple(
        pl.pallas_call(
            parted_kernel,
            out_shape=[shaped(w_in.shape, f32), shaped(w_out.shape, f32)],
            compiler_params=params(),
            name="parted",
        )(total)
    )


def solution(mesh):
    fine = Mesh(mesh.devices.reshape(4, 8, 4, 2), EVERY)
    lat, member = ("x", "z"), MEMBER
    return jax.shard_map(
        body,
        mesh=fine,
        in_specs=(
            P(member, lat, None, None),
            P(),
            P(member, lat, None, None),
            P(member, None, None),
            P(member, None, None),
            P(lat, None, None),
            P(),
        ),
        out_specs=(P(member, None, None), P(member, None, None)),
        check_vma=False,
    )
```

```python
import functools
import math

import jax
import jax.numpy as jnp
import numpy as np
from jax import lax
from jax.experimental import pallas as pl
from jax.experimental.pallas import tpu as pltpu
from jax.sharding import Mesh, PartitionSpec as P

LAT = 256
STEPS = 3

EVERY = ("x", "z", "y", "core")
PLANE = ("x", "y", "core")
MEMBER = ("y", "core")

PAIR = 2
SHARE = 8
VMEM = 24 * 1024 * 1024
MOST = 58 * 1024 * 1024


def fourier_matrix(longitudes, orders):
    points = np.arange(longitudes, dtype=np.int32)[:, None]
    angles = (2.0 * math.pi / longitudes * (points * orders[None, :] % longitudes)).astype(
        np.float32
    )
    factor = math.sqrt(2.0 / longitudes)
    paired = np.stack([factor * np.cos(angles), -factor * np.sin(angles)], axis=2)
    return paired.astype(np.float32).reshape(longitudes, 2 * orders.shape[0])


def across(left, right):
    return lax.dot_general(
        left, right, (((0,), (0,)), ((), ())), preferred_element_type=jnp.float32
    )


def exchange(values, axes):
    return lax.all_to_all(values, axes, split_axis=0, concat_axis=0, tiled=True)


def dot(left, right):
    return jnp.dot(left, right, preferred_element_type=jnp.float32)


def row_of(wide, row, rows):
    return wide[pl.ds(row, wide.shape[0] // rows, stride=rows), :]


def side_by_side(parts):
    return jnp.concatenate(parts, axis=1)


def to_grid(wide, fourier, first, rows):
    lines = [row_of(wide, first + i, rows).astype(jnp.bfloat16) for i in range(PAIR)]
    grid = dot(fourier[...], side_by_side(lines))
    return [grid[:, i * 128 : (i + 1) * 128] for i in range(PAIR)]


def to_modes(wide, turned, fields, first, rows):
    spectra = dot(turned[...], side_by_side(fields))
    for i in range(PAIR):
        wide[pl.ds(first + i, spectra.shape[0], stride=rows), :] = spectra[
            :, i * 128 : (i + 1) * 128
        ]


def network(current, w_in, w_out, low_ref, hidden_ref, moved_ref, row):
    low = current.astype(jnp.bfloat16)
    hidden = jnp.tanh(dot(low, w_in[...])).astype(jnp.bfloat16)
    moved = current + dot(hidden, w_out[...])
    low_ref[row] = low
    hidden_ref[row] = hidden
    moved_ref[row] = moved
    return moved.astype(jnp.bfloat16)


def by_pairs(rows):
    def wrapped(run):
        for first in range(0, rows, PAIR):
            run(first)

    return wrapped


def start_kernel(rows, frame, turned, w_in, w_out, spectra, moved, low, hidden, wide):
    @by_pairs(rows)
    def _(first):
        fields = [
            network(frame[row].astype(jnp.float32), w_in, w_out, low, hidden, moved, row)
            for row in range(first, first + PAIR)
        ]
        to_modes(wide, turned, fields, first, rows)

    spectra[...] = wide[...].astype(jnp.bfloat16)


def ahead_kernel(rows, last, returned, before, fourier, turned, w_in, w_out, *rest):
    if last:
        aim, spectra, moved, low, hidden, back, wide = rest
    else:
        spectra, moved, low, hidden, back, wide = rest
    back[...] = returned[...].astype(jnp.float32)

    @by_pairs(rows)
    def _(first):
        grid = to_grid(back, fourier, first, rows)
        fields = [
            network(before[first + i] - grid[i], w_in, w_out, low, hidden, moved, first + i)
            for i in range(PAIR)
        ]
        to_modes(wide, turned, fields, first, rows)

    if last:
        owners = spectra.shape[0]
        spectra[:, 0] = wide[...].astype(jnp.bfloat16).reshape(owners, -1, 128)
        spectra[:, 1] = aim[...].reshape(owners, -1, 128)
    else:
        spectra[...] = wide[...].astype(jnp.bfloat16)


def aim_kernel(rows, target, turned, spectra, wide):
    @by_pairs(rows)
    def _(first):
        to_modes(wide, turned, [target[first + i] for i in range(PAIR)], first, rows)

    spectra[...] = wide[...].astype(jnp.bfloat16)


def adjoint_kernel(rows, first_one, last, returned, base, *rest):
    rest = list(rest)
    target = rest.pop(0) if first_one else None
    low, hidden, fourier, out_t = rest[:4]
    rest = rest[4:]
    if last:
        sum_in, sum_out, sums, back, total_in, total_out = rest
    else:
        turned, in_t = rest[:2]
        rest = rest[2:]
        if first_one:
            sum_in = sum_out = None
        else:
            sum_in, sum_out = rest[:2]
            rest = rest[2:]
        spectra, adjoint, total_in, total_out, back, wide = rest
    back[...] = returned[...].astype(jnp.float32)
    if first_one:
        total_in[...] = jnp.zeros_like(total_in)
        total_out[...] = jnp.zeros_like(total_out)
    else:
        total_in[...] = sum_in[...]
        total_out[...] = sum_out[...]

    @by_pairs(rows)
    def _(first):
        grid = to_grid(back, fourier, first, rows)
        fields = []
        for i in range(PAIR):
            row = first + i
            if first_one:
                pulled = (base[row] - target[row].astype(jnp.float32) - grid[i]) * (1.0 / LAT)
            else:
                pulled = base[row] - grid[i]
            pulled_low = pulled.astype(jnp.bfloat16)
            units = hidden[row]
            total_out[...] += across(pulled_low, units)
            wide_units = units.astype(jnp.float32)
            inner = (dot(pulled_low, out_t[...]) * (1.0 - wide_units * wide_units)).astype(
                jnp.bfloat16
            )
            total_in[...] += across(low[row], inner)
            if not last:
                value = pulled + dot(inner, in_t[...])
                adjoint[row] = value
                fields.append(value.astype(jnp.bfloat16))
        if not last:
            to_modes(wide, turned, fields, first, rows)

    if last:
        height = total_in.shape[0]
        halves = total_in.shape[1] // 128
        for h in range(halves):
            part = slice(h * 128, (h + 1) * 128)
            sums[h * height : (h + 1) * height] = total_in[:, part]
            sums[(halves + h) * height : (halves + h + 1) * height] = total_out[:, part].T
    else:
        spectra[...] = wide[...].astype(jnp.bfloat16)


def parted_kernel(total, grad_in, grad_out):
    height = grad_in.shape[1]
    halves = grad_in.shape[2] // 128
    for h in range(halves):
        grad_in[0, :, h * 128 : (h + 1) * 128] = total[h * height : (h + 1) * height]
    grad_out[0] = total[halves * height :]


def gather_lines(block, k):
    values = block[:, k].astype(jnp.float32)
    owners, pair, channels = values.shape
    values = values.reshape(owners, 2, pair // 2, channels)
    return side_by_side([values[:, r].reshape(-1, channels) for r in range(2)])


def scatter_lines(out, k, values):
    owners = out.shape[0]
    halves = [values[:, r * 128 : (r + 1) * 128].reshape(owners, 1, -1, 128) for r in range(2)]
    lines = jnp.concatenate(halves, axis=1)
    out[:, k] = lines.reshape(owners, -1, 128).astype(jnp.bfloat16)


def filtered(spectra, table, turned, damping):
    coefficients = (dot(turned, spectra) * damping[...]).astype(jnp.bfloat16)
    return dot(table, coefficients)


def filter_kernel(received, table, turned, damping, out):
    @pl.loop(0, table.shape[0], step=SHARE)
    def _(first):
        for k in [first + i for i in range(SHARE)]:
            spectra = gather_lines(received, k).astype(jnp.bfloat16)
            scatter_lines(out, k, filtered(spectra, table[k], turned[k], damping))


def filter_twice_kernel(received, norms, table, turned, damping, out):
    @pl.loop(0, table.shape[0], step=SHARE)
    def _(start):
        for k in [start + i for i in range(SHARE)]:
            spectra = gather_lines(received.at[:, 0], k)
            first = filtered(spectra.astype(jnp.bfloat16), table[k], turned[k], damping)
            second = 2.0 * spectra - gather_lines(received.at[:, 1], k) - norms[k] * first
            scatter_lines(
                out, k, filtered(second.astype(jnp.bfloat16), table[k], turned[k], damping)
            )


def params(limit=VMEM):
    return pltpu.CompilerParams(vmem_limit_bytes=limit)


def shaped(shape, dtype):
    return jax.ShapeDtypeStruct(shape, dtype)


def in_smem():
    return pl.BlockSpec(memory_space=pltpu.SMEM)


def anywhere():
    return pl.BlockSpec(memory_space=pl.ANY)


def in_vmem():
    return pl.BlockSpec(memory_space=pltpu.VMEM)


def paired_kernel(first, second, after, out, slots, in_sems, out_sems):
    places = [(p, s) for p in range(2) for s in range(first.shape[0])]
    ins, outs = [], []
    for p, s in places:
        source = (first, second)[p].at[s]
        ins.append(pltpu.make_async_copy(source, slots.at[s, p], in_sems.at[p, s]))
        outs.append(pltpu.make_async_copy(slots.at[s, p], out.at[s, p], out_sems.at[p, s]))
    for copy in ins:
        copy.start()
    for copy, after in zip(ins, outs):
        copy.wait()
        after.start()
    for copy in outs:
        copy.wait()


def paired(first, second, after):
    rows = first.shape[0]
    shape = (rows, 2) + first.shape[1:]
    return pl.pallas_call(
        paired_kernel,
        in_specs=[anywhere()] * 3,
        out_specs=anywhere(),
        out_shape=shaped(shape, first.dtype),
        scratch_shapes=[
            pltpu.VMEM(shape, first.dtype),
            pltpu.SemaphoreType.DMA((2, rows)),
            pltpu.SemaphoreType.DMA((2, rows)),
        ],
        compiler_params=params(MOST),
        name="paired",
    )(first, second, after)


def chosen_kernel(window, both, frame, held):
    for k in range(frame.shape[0]):
        frame[k] = both[window[k], 0]
        held[k] = both[k, 1]


def chosen(window, both):
    members = both.shape[0]
    out = shaped((members,) + both.shape[2:], both.dtype)
    return pl.pallas_call(
        chosen_kernel,
        in_specs=[in_smem(), in_vmem()],
        out_specs=[in_vmem()] * 2,
        out_shape=[out, out],
        compiler_params=params(),
        name="chosen",
    )(jnp.clip(window, 0, members - 1), both)


def body(frames, window, targets, w_in, w_out, legendre, damping):
    rows, longitudes, channels = frames.shape[1:]
    units = w_in.shape[2]
    size_x, size_z = lax.axis_size("x"), lax.axis_size("z")
    members = lax.axis_size(MEMBER)
    owners = size_x * members
    modes = legendre.shape[0]
    degrees = legendre.shape[2]
    lines = owners * 2 * modes * rows
    width = 2 * modes * owners
    place = lax.axis_index(MEMBER)
    plane = lax.axis_index("z")
    bf16, f32 = jnp.bfloat16, jnp.float32

    swap = [
        ((x * size_z + z) * members + k, (x * size_z + k) * members + z)
        for x in range(size_x)
        for z in range(size_z)
        for k in range(members)
    ]
    first_layer = lax.ppermute(w_in[0], EVERY, swap)
    second_layer = lax.ppermute(w_out[0], EVERY, swap)

    table = lax.dynamic_index_in_dim(legendre, place, 0, keepdims=False)
    table = table.reshape(size_x, size_z, rows, degrees)
    table = table.transpose(0, 2, 1, 3).reshape(owners * rows, degrees)
    both = paired(frames[0], targets[0], table)
    table = lax.all_gather(table, "z")

    both = exchange(both, MEMBER)
    both, first_layer, second_layer = lax.optimization_barrier((both, first_layer, second_layer))
    frame, held = chosen(window, both)
    frame = exchange(frame, "z")
    held, frame, table = lax.optimization_barrier((held, frame, table))
    held = lax.all_gather(held, "z")

    table = table.reshape(modes, owners * rows, degrees)
    turned_table = table.transpose(0, 2, 1)

    ordered = np.arange(modes * owners, dtype=np.int32)
    ordered = ordered.reshape(size_x, size_z, members).transpose(0, 2, 1).reshape(-1)
    matrix = fourier_matrix(longitudes, ordered)
    fourier = jnp.asarray(matrix).astype(bf16)
    turned = jnp.asarray(np.ascontiguousarray(matrix.T)).astype(bf16)

    mode = (lax.axis_index("x") * size_z + jnp.arange(modes)) * members + place
    norms = jnp.where(mode[:, None] == 0, jnp.array([[2.0, 0.0]]), 1.0)
    norms = jnp.repeat(norms, channels, axis=1).reshape(modes, 1, 2 * channels)
    decay = jnp.broadcast_to(damping[:, None], (degrees, 2 * channels))

    shape = (rows, longitudes, channels)
    deep_shape = (rows, longitudes, units)
    buffer = pltpu.VMEM((lines, channels), f32)

    def forward(returned, before, aim=None):
        last = aim is not None
        if returned is None:
            kernel = functools.partial(start_kernel, rows)
            operands = [before, turned, first_layer, second_layer]
            scratch = [buffer]
        else:
            kernel = functools.partial(ahead_kernel, rows, last)
            operands = [returned, before, fourier, turned, first_layer, second_layer]
            operands += [aim] if last else []
            scratch = [buffer, buffer]
        cells = rows * longitudes
        return pl.pallas_call(
            kernel,
            out_shape=[
                shaped((owners, 2, lines // owners, channels) if last else (lines, channels), bf16),
                shaped(shape, f32),
                shaped(shape, bf16),
                shaped(deep_shape, bf16),
            ],
            scratch_shapes=scratch,
            compiler_params=params(),
            cost_estimate=pl.CostEstimate(
                flops=4 * cells * channels * (units + width),
                bytes_accessed=9 * cells * channels * 2,
                transcendentals=cells * units,
            ),
            name="forward",
        )(*operands)

    def transformed(target):
        return pl.pallas_call(
            functools.partial(aim_kernel, rows),
            out_shape=shaped((lines, channels), bf16),
            scratch_shapes=[buffer],
            compiler_params=params(),
            cost_estimate=pl.CostEstimate(
                flops=2 * rows * longitudes * channels * width,
                bytes_accessed=4 * lines * channels,
                transcendentals=0,
            ),
            name="aim",
        )(target, turned)

    def adjoint_of(returned, base, low, hidden, sums, target=None, last=False):
        first_one = target is not None
        operands = [returned, base] + ([target] if first_one else [])
        operands += [low, hidden, fourier, out_t]
        sum_shape = shaped(first_layer.shape, f32)
        accumulators = [pltpu.VMEM(first_layer.shape, f32)] * 2
        if last:
            operands += list(sums)
            outs = shaped((2 * units, channels), f32)
            scratch = [buffer] + accumulators
        else:
            operands += [turned, in_t] + ([] if first_one else list(sums))
            outs = [shaped((lines, channels), bf16), shaped(shape, f32), sum_shape, sum_shape]
            scratch = [buffer, buffer]
        cells = rows * longitudes
        return pl.pallas_call(
            functools.partial(adjoint_kernel, rows, first_one, last),
            out_shape=outs,
            scratch_shapes=scratch,
            compiler_params=params(),
            cost_estimate=pl.CostEstimate(
                flops=4 * cells * channels * (2 * units + width),
                bytes_accessed=11 * cells * channels * 2,
                transcendentals=0,
            ),
            name="adjoint",
        )(*operands)

    blocks = (owners, modes, 2 * rows, channels)

    def filtering(received):
        out = pl.pallas_call(
            filter_kernel,
            out_shape=shaped(blocks, bf16),
            compiler_params=params(),
            cost_estimate=pl.CostEstimate(
                flops=8 * lines * channels * degrees,
                bytes_accessed=8 * lines * channels,
                transcendentals=0,
            ),
            name="filter",
        )(received.reshape(blocks), table, turned_table, decay)
        return out.reshape(lines, channels)

    def filtering_twice(received):
        received = received.reshape(owners, 2, modes, 2 * rows, channels)
        out = pl.pallas_call(
            filter_twice_kernel,
            out_shape=shaped(blocks, bf16),
            compiler_params=params(),
            cost_estimate=pl.CostEstimate(
                flops=16 * lines * channels * degrees,
                bytes_accessed=10 * lines * channels,
                transcendentals=0,
            ),
            name="filter_twice",
        )(received, norms, table, turned_table, decay)
        return out.reshape(lines, channels)

    in_t, out_t = first_layer.T, second_layer.T
    table, turned_table, decay, norms, in_t, out_t, first_layer, second_layer, frame = (
        lax.optimization_barrier(
            (table, turned_table, decay, norms, in_t, out_t, first_layer, second_layer, frame)
        )
    )
    history = []
    moved, returned, aim = frame, None, None
    for step in range(STEPS):
        if step == STEPS - 1:
            held, returned = lax.optimization_barrier((held, returned))
            target = lax.dynamic_index_in_dim(held, plane, 1, keepdims=False)
            aim = transformed(target)
        spectra, moved, low, hidden = forward(returned, moved, aim)
        history.append((low, hidden))
        if step < STEPS - 1:
            returned = exchange(filtering(exchange(spectra, PLANE)), PLANE)
    received = exchange(spectra, PLANE)
    returned = exchange(filtering_twice(received), PLANE)

    sums = None
    adjoint = moved
    for step in reversed(range(1, STEPS)):
        low, hidden = history[step]
        spectra, adjoint, *sums = adjoint_of(
            returned, adjoint, low, hidden, sums, target if step == STEPS - 1 else None
        )
        returned = exchange(filtering(exchange(spectra, PLANE)), PLANE)
    low, hidden = history[0]
    sums = adjoint_of(returned, adjoint, low, hidden, sums, None, True)

    height = sums.shape[0] // owners
    pieces = exchange(sums, PLANE).reshape(owners, height, 128).sum(axis=0)
    around = exchange(jnp.broadcast_to(pieces[None], (size_z, height, 128)), "z")
    spread = jnp.broadcast_to(around[None], (size_x, members, height, 128))
    total = exchange(spread.reshape(-1, 128), PLANE)
    return tuple(
        pl.pallas_call(
            parted_kernel,
            out_shape=[shaped(w_in.shape, f32), shaped(w_out.shape, f32)],
            compiler_params=params(),
            name="parted",
        )(total)
    )


def solution(mesh):
    fine = Mesh(mesh.devices.reshape(4, 8, 4, 2), EVERY)
    lat, member = ("x", "z"), MEMBER
    return jax.shard_map(
        body,
        mesh=fine,
        in_specs=(
            P(member, lat, None, None),
            P(),
            P(member, lat, None, None),
            P(member, None, None),
            P(member, None, None),
            P(lat, None, None),
            P(),
        ),
        out_specs=(P(member, None, None), P(member, None, None)),
        check_vma=False,
    )
```

```python
import functools
import math

import jax
import jax.numpy as jnp
import numpy as np
from jax import lax
from jax.experimental import pallas as pl
from jax.experimental.pallas import tpu as pltpu
from jax.sharding import Mesh, PartitionSpec as P

LAT = 256
STEPS = 3

EVERY = ("x", "z", "y", "core")
PLANE = ("x", "y", "core")
MEMBER = ("y", "core")

PAIR = 4
SHARE = 8
VMEM = 24 * 1024 * 1024
MOST = 58 * 1024 * 1024


def fourier_matrix(longitudes, orders):
    points = np.arange(longitudes, dtype=np.int32)[:, None]
    angles = (2.0 * math.pi / longitudes * (points * orders[None, :] % longitudes)).astype(
        np.float32
    )
    factor = math.sqrt(2.0 / longitudes)
    paired = np.stack([factor * np.cos(angles), -factor * np.sin(angles)], axis=2)
    return paired.astype(np.float32).reshape(longitudes, 2 * orders.shape[0])


def across(left, right):
    return lax.dot_general(
        left, right, (((0,), (0,)), ((), ())), preferred_element_type=jnp.float32
    )


def exchange(values, axes):
    return lax.all_to_all(values, axes, split_axis=0, concat_axis=0, tiled=True)


def dot(left, right):
    return jnp.dot(left, right, preferred_element_type=jnp.float32)


def row_of(wide, row, rows):
    return wide[pl.ds(row, wide.shape[0] // rows, stride=rows), :]


def side_by_side(parts):
    return jnp.concatenate(parts, axis=1)


def to_grid(wide, fourier, first, rows):
    lines = [row_of(wide, first + i, rows).astype(jnp.bfloat16) for i in range(PAIR)]
    grid = dot(fourier[...], side_by_side(lines))
    return [grid[:, i * 128 : (i + 1) * 128] for i in range(PAIR)]


def to_modes(wide, turned, fields, first, rows):
    spectra = dot(turned[...], side_by_side(fields))
    for i in range(PAIR):
        wide[pl.ds(first + i, spectra.shape[0], stride=rows), :] = spectra[
            :, i * 128 : (i + 1) * 128
        ]


def network(current, w_in, w_out, low_ref, hidden_ref, moved_ref, row):
    low = current.astype(jnp.bfloat16)
    hidden = jnp.tanh(dot(low, w_in[...])).astype(jnp.bfloat16)
    moved = current + dot(hidden, w_out[...])
    low_ref[row] = low
    hidden_ref[row] = hidden
    moved_ref[row] = moved
    return moved.astype(jnp.bfloat16)


def by_pairs(rows):
    def wrapped(run):
        for first in range(0, rows, PAIR):
            run(first)

    return wrapped


def start_kernel(rows, frame, turned, w_in, w_out, spectra, moved, low, hidden, wide):
    @by_pairs(rows)
    def _(first):
        fields = [
            network(frame[row].astype(jnp.float32), w_in, w_out, low, hidden, moved, row)
            for row in range(first, first + PAIR)
        ]
        to_modes(wide, turned, fields, first, rows)

    spectra[...] = wide[...].astype(jnp.bfloat16)


def ahead_kernel(rows, last, returned, before, fourier, turned, w_in, w_out, *rest):
    if last:
        aim, spectra, moved, low, hidden, back, wide = rest
    else:
        spectra, moved, low, hidden, back, wide = rest
    back[...] = returned[...].astype(jnp.float32)

    @by_pairs(rows)
    def _(first):
        grid = to_grid(back, fourier, first, rows)
        fields = [
            network(before[first + i] - grid[i], w_in, w_out, low, hidden, moved, first + i)
            for i in range(PAIR)
        ]
        to_modes(wide, turned, fields, first, rows)

    if last:
        owners = spectra.shape[0]
        spectra[:, 0] = wide[...].astype(jnp.bfloat16).reshape(owners, -1, 128)
        spectra[:, 1] = aim[...].reshape(owners, -1, 128)
    else:
        spectra[...] = wide[...].astype(jnp.bfloat16)


def aim_kernel(rows, target, turned, spectra, wide):
    @by_pairs(rows)
    def _(first):
        to_modes(wide, turned, [target[first + i] for i in range(PAIR)], first, rows)

    spectra[...] = wide[...].astype(jnp.bfloat16)


def adjoint_kernel(rows, first_one, last, returned, base, *rest):
    rest = list(rest)
    target = rest.pop(0) if first_one else None
    low, hidden, fourier, out_t = rest[:4]
    rest = rest[4:]
    if last:
        sum_in, sum_out, sums, back, total_in, total_out = rest
    else:
        turned, in_t = rest[:2]
        rest = rest[2:]
        if first_one:
            sum_in = sum_out = None
        else:
            sum_in, sum_out = rest[:2]
            rest = rest[2:]
        spectra, adjoint, total_in, total_out, back, wide = rest
    back[...] = returned[...].astype(jnp.float32)
    if first_one:
        total_in[...] = jnp.zeros_like(total_in)
        total_out[...] = jnp.zeros_like(total_out)
    else:
        total_in[...] = sum_in[...]
        total_out[...] = sum_out[...]

    @by_pairs(rows)
    def _(first):
        grid = to_grid(back, fourier, first, rows)
        fields = []
        for i in range(PAIR):
            row = first + i
            if first_one:
                pulled = (base[row] - target[row].astype(jnp.float32) - grid[i]) * (1.0 / LAT)
            else:
                pulled = base[row] - grid[i]
            pulled_low = pulled.astype(jnp.bfloat16)
            units = hidden[row]
            total_out[...] += across(pulled_low, units)
            wide_units = units.astype(jnp.float32)
            inner = (dot(pulled_low, out_t[...]) * (1.0 - wide_units * wide_units)).astype(
                jnp.bfloat16
            )
            total_in[...] += across(low[row], inner)
            if not last:
                value = pulled + dot(inner, in_t[...])
                adjoint[row] = value
                fields.append(value.astype(jnp.bfloat16))
        if not last:
            to_modes(wide, turned, fields, first, rows)

    if last:
        height = total_in.shape[0]
        halves = total_in.shape[1] // 128
        for h in range(halves):
            part = slice(h * 128, (h + 1) * 128)
            sums[h * height : (h + 1) * height] = total_in[:, part]
            sums[(halves + h) * height : (halves + h + 1) * height] = total_out[:, part].T
    else:
        spectra[...] = wide[...].astype(jnp.bfloat16)


def parted_kernel(total, grad_in, grad_out):
    height = grad_in.shape[1]
    halves = grad_in.shape[2] // 128
    for h in range(halves):
        grad_in[0, :, h * 128 : (h + 1) * 128] = total[h * height : (h + 1) * height]
    grad_out[0] = total[halves * height :]


def gather_lines(block, k):
    values = block[:, k].astype(jnp.float32)
    owners, pair, channels = values.shape
    values = values.reshape(owners, 2, pair // 2, channels)
    return side_by_side([values[:, r].reshape(-1, channels) for r in range(2)])


def scatter_lines(out, k, values):
    owners = out.shape[0]
    halves = [values[:, r * 128 : (r + 1) * 128].reshape(owners, 1, -1, 128) for r in range(2)]
    lines = jnp.concatenate(halves, axis=1)
    out[:, k] = lines.reshape(owners, -1, 128).astype(jnp.bfloat16)


def filtered(spectra, table, turned, damping):
    coefficients = (dot(turned, spectra) * damping[...]).astype(jnp.bfloat16)
    return dot(table, coefficients)


def filter_kernel(received, table, turned, damping, out):
    @pl.loop(0, table.shape[0], step=SHARE)
    def _(first):
        for k in [first + i for i in range(SHARE)]:
            spectra = gather_lines(received, k).astype(jnp.bfloat16)
            scatter_lines(out, k, filtered(spectra, table[k], turned[k], damping))


def filter_twice_kernel(received, norms, table, turned, damping, out):
    @pl.loop(0, table.shape[0], step=SHARE)
    def _(start):
        for k in [start + i for i in range(SHARE)]:
            spectra = gather_lines(received.at[:, 0], k)
            first = filtered(spectra.astype(jnp.bfloat16), table[k], turned[k], damping)
            second = 2.0 * spectra - gather_lines(received.at[:, 1], k) - norms[k] * first
            scatter_lines(
                out, k, filtered(second.astype(jnp.bfloat16), table[k], turned[k], damping)
            )


def params(limit=VMEM):
    return pltpu.CompilerParams(vmem_limit_bytes=limit)


def shaped(shape, dtype):
    return jax.ShapeDtypeStruct(shape, dtype)


def in_smem():
    return pl.BlockSpec(memory_space=pltpu.SMEM)


def anywhere():
    return pl.BlockSpec(memory_space=pl.ANY)


def in_vmem():
    return pl.BlockSpec(memory_space=pltpu.VMEM)


def paired_kernel(first, second, after, out, slots, in_sems, out_sems):
    places = [(p, s) for p in range(2) for s in range(first.shape[0])]
    ins, outs = [], []
    for p, s in places:
        source = (first, second)[p].at[s]
        ins.append(pltpu.make_async_copy(source, slots.at[s, p], in_sems.at[p, s]))
        outs.append(pltpu.make_async_copy(slots.at[s, p], out.at[s, p], out_sems.at[p, s]))
    for copy in ins:
        copy.start()
    for copy, after in zip(ins, outs):
        copy.wait()
        after.start()
    for copy in outs:
        copy.wait()


def paired(first, second, after):
    rows = first.shape[0]
    shape = (rows, 2) + first.shape[1:]
    return pl.pallas_call(
        paired_kernel,
        in_specs=[anywhere()] * 3,
        out_specs=anywhere(),
        out_shape=shaped(shape, first.dtype),
        scratch_shapes=[
            pltpu.VMEM(shape, first.dtype),
            pltpu.SemaphoreType.DMA((2, rows)),
            pltpu.SemaphoreType.DMA((2, rows)),
        ],
        compiler_params=params(MOST),
        name="paired",
    )(first, second, after)


def chosen_kernel(window, both, frame, held):
    for k in range(frame.shape[0]):
        frame[k] = both[window[k], 0]
        held[k] = both[k, 1]


def chosen(window, both):
    members = both.shape[0]
    out = shaped((members,) + both.shape[2:], both.dtype)
    return pl.pallas_call(
        chosen_kernel,
        in_specs=[in_smem(), in_vmem()],
        out_specs=[in_vmem()] * 2,
        out_shape=[out, out],
        compiler_params=params(),
        name="chosen",
    )(jnp.clip(window, 0, members - 1), both)


def body(frames, window, targets, w_in, w_out, legendre, damping):
    rows, longitudes, channels = frames.shape[1:]
    units = w_in.shape[2]
    size_x, size_z = lax.axis_size("x"), lax.axis_size("z")
    members = lax.axis_size(MEMBER)
    owners = size_x * members
    modes = legendre.shape[0]
    degrees = legendre.shape[2]
    lines = owners * 2 * modes * rows
    width = 2 * modes * owners
    place = lax.axis_index(MEMBER)
    plane = lax.axis_index("z")
    bf16, f32 = jnp.bfloat16, jnp.float32

    swap = [
        ((x * size_z + z) * members + k, (x * size_z + k) * members + z)
        for x in range(size_x)
        for z in range(size_z)
        for k in range(members)
    ]
    first_layer = lax.ppermute(w_in[0], EVERY, swap)
    second_layer = lax.ppermute(w_out[0], EVERY, swap)

    table = lax.dynamic_index_in_dim(legendre, place, 0, keepdims=False)
    table = table.reshape(size_x, size_z, rows, degrees)
    table = table.transpose(0, 2, 1, 3).reshape(owners * rows, degrees)
    both = paired(frames[0], targets[0], table)
    table = lax.all_gather(table, "z")

    both = exchange(both, MEMBER)
    both, first_layer, second_layer = lax.optimization_barrier((both, first_layer, second_layer))
    frame, held = chosen(window, both)
    frame = exchange(frame, "z")
    held, frame, table = lax.optimization_barrier((held, frame, table))
    held = lax.all_gather(held, "z")

    table = table.reshape(modes, owners * rows, degrees)
    turned_table = table.transpose(0, 2, 1)

    ordered = np.arange(modes * owners, dtype=np.int32)
    ordered = ordered.reshape(size_x, size_z, members).transpose(0, 2, 1).reshape(-1)
    matrix = fourier_matrix(longitudes, ordered)
    fourier = jnp.asarray(matrix).astype(bf16)
    turned = jnp.asarray(np.ascontiguousarray(matrix.T)).astype(bf16)

    mode = (lax.axis_index("x") * size_z + jnp.arange(modes)) * members + place
    norms = jnp.where(mode[:, None] == 0, jnp.array([[2.0, 0.0]]), 1.0)
    norms = jnp.repeat(norms, channels, axis=1).reshape(modes, 1, 2 * channels)
    decay = jnp.broadcast_to(damping[:, None], (degrees, 2 * channels))

    shape = (rows, longitudes, channels)
    deep_shape = (rows, longitudes, units)
    buffer = pltpu.VMEM((lines, channels), f32)

    def forward(returned, before, aim=None):
        last = aim is not None
        if returned is None:
            kernel = functools.partial(start_kernel, rows)
            operands = [before, turned, first_layer, second_layer]
            scratch = [buffer]
        else:
            kernel = functools.partial(ahead_kernel, rows, last)
            operands = [returned, before, fourier, turned, first_layer, second_layer]
            operands += [aim] if last else []
            scratch = [buffer, buffer]
        cells = rows * longitudes
        return pl.pallas_call(
            kernel,
            out_shape=[
                shaped((owners, 2, lines // owners, channels) if last else (lines, channels), bf16),
                shaped(shape, f32),
                shaped(shape, bf16),
                shaped(deep_shape, bf16),
            ],
            scratch_shapes=scratch,
            compiler_params=params(),
            cost_estimate=pl.CostEstimate(
                flops=4 * cells * channels * (units + width),
                bytes_accessed=9 * cells * channels * 2,
                transcendentals=cells * units,
            ),
            name="forward",
        )(*operands)

    def transformed(target):
        return pl.pallas_call(
            functools.partial(aim_kernel, rows),
            out_shape=shaped((lines, channels), bf16),
            scratch_shapes=[buffer],
            compiler_params=params(),
            cost_estimate=pl.CostEstimate(
                flops=2 * rows * longitudes * channels * width,
                bytes_accessed=4 * lines * channels,
                transcendentals=0,
            ),
            name="aim",
        )(target, turned)

    def adjoint_of(returned, base, low, hidden, sums, target=None, last=False):
        first_one = target is not None
        operands = [returned, base] + ([target] if first_one else [])
        operands += [low, hidden, fourier, out_t]
        sum_shape = shaped(first_layer.shape, f32)
        accumulators = [pltpu.VMEM(first_layer.shape, f32)] * 2
        if last:
            operands += list(sums)
            outs = shaped((2 * units, channels), f32)
            scratch = [buffer] + accumulators
        else:
            operands += [turned, in_t] + ([] if first_one else list(sums))
            outs = [shaped((lines, channels), bf16), shaped(shape, f32), sum_shape, sum_shape]
            scratch = [buffer, buffer]
        cells = rows * longitudes
        return pl.pallas_call(
            functools.partial(adjoint_kernel, rows, first_one, last),
            out_shape=outs,
            scratch_shapes=scratch,
            compiler_params=params(),
            cost_estimate=pl.CostEstimate(
                flops=4 * cells * channels * (2 * units + width),
                bytes_accessed=11 * cells * channels * 2,
                transcendentals=0,
            ),
            name="adjoint",
        )(*operands)

    blocks = (owners, modes, 2 * rows, channels)

    def filtering(received):
        out = pl.pallas_call(
            filter_kernel,
            out_shape=shaped(blocks, bf16),
            compiler_params=params(),
            cost_estimate=pl.CostEstimate(
                flops=8 * lines * channels * degrees,
                bytes_accessed=8 * lines * channels,
                transcendentals=0,
            ),
            name="filter",
        )(received.reshape(blocks), table, turned_table, decay)
        return out.reshape(lines, channels)

    def filtering_twice(received):
        received = received.reshape(owners, 2, modes, 2 * rows, channels)
        out = pl.pallas_call(
            filter_twice_kernel,
            out_shape=shaped(blocks, bf16),
            compiler_params=params(),
            cost_estimate=pl.CostEstimate(
                flops=16 * lines * channels * degrees,
                bytes_accessed=10 * lines * channels,
                transcendentals=0,
            ),
            name="filter_twice",
        )(received, norms, table, turned_table, decay)
        return out.reshape(lines, channels)

    in_t, out_t = first_layer.T, second_layer.T
    table, turned_table, decay, norms, in_t, out_t, first_layer, second_layer, frame = (
        lax.optimization_barrier(
            (table, turned_table, decay, norms, in_t, out_t, first_layer, second_layer, frame)
        )
    )
    history = []
    moved, returned, aim = frame, None, None
    for step in range(STEPS):
        if step == STEPS - 1:
            held, returned = lax.optimization_barrier((held, returned))
            target = lax.dynamic_index_in_dim(held, plane, 1, keepdims=False)
            aim = transformed(target)
        spectra, moved, low, hidden = forward(returned, moved, aim)
        history.append((low, hidden))
        if step < STEPS - 1:
            returned = exchange(filtering(exchange(spectra, PLANE)), PLANE)
    received = exchange(spectra, PLANE)
    returned = exchange(filtering_twice(received), PLANE)

    sums = None
    adjoint = moved
    for step in reversed(range(1, STEPS)):
        low, hidden = history[step]
        spectra, adjoint, *sums = adjoint_of(
            returned, adjoint, low, hidden, sums, target if step == STEPS - 1 else None
        )
        returned = exchange(filtering(exchange(spectra, PLANE)), PLANE)
    low, hidden = history[0]
    sums = adjoint_of(returned, adjoint, low, hidden, sums, None, True)

    height = sums.shape[0] // owners
    pieces = exchange(sums, PLANE).reshape(owners, height, 128).sum(axis=0)
    around = exchange(jnp.broadcast_to(pieces[None], (size_z, height, 128)), "z")
    spread = jnp.broadcast_to(around[None], (size_x, members, height, 128))
    total = exchange(spread.reshape(-1, 128), PLANE)
    return tuple(
        pl.pallas_call(
            parted_kernel,
            out_shape=[shaped(w_in.shape, f32), shaped(w_out.shape, f32)],
            compiler_params=params(),
            name="parted",
        )(total)
    )


def solution(mesh):
    fine = Mesh(mesh.devices.reshape(4, 8, 4, 2), EVERY)
    lat, member = ("x", "z"), MEMBER
    return jax.shard_map(
        body,
        mesh=fine,
        in_specs=(
            P(member, lat, None, None),
            P(),
            P(member, lat, None, None),
            P(member, None, None),
            P(member, None, None),
            P(lat, None, None),
            P(),
        ),
        out_specs=(P(member, None, None), P(member, None, None)),
        check_vma=False,
    )
```

```python
import functools
import math

import jax
import jax.numpy as jnp
import numpy as np
from jax import lax
from jax.experimental import pallas as pl
from jax.experimental.pallas import tpu as pltpu
from jax.sharding import Mesh, PartitionSpec as P

LAT = 256
STEPS = 3

EVERY = ("x", "z", "y", "core")
PLANE = ("x", "y", "core")
MEMBER = ("y", "core")

PAIR = 8
SHARE = 8
VMEM = 24 * 1024 * 1024
MOST = 58 * 1024 * 1024


def fourier_matrix(longitudes, orders):
    points = np.arange(longitudes, dtype=np.int32)[:, None]
    angles = (2.0 * math.pi / longitudes * (points * orders[None, :] % longitudes)).astype(
        np.float32
    )
    factor = math.sqrt(2.0 / longitudes)
    paired = np.stack([factor * np.cos(angles), -factor * np.sin(angles)], axis=2)
    return paired.astype(np.float32).reshape(longitudes, 2 * orders.shape[0])


def across(left, right):
    return lax.dot_general(
        left, right, (((0,), (0,)), ((), ())), preferred_element_type=jnp.float32
    )


def exchange(values, axes):
    return lax.all_to_all(values, axes, split_axis=0, concat_axis=0, tiled=True)


def dot(left, right):
    return jnp.dot(left, right, preferred_element_type=jnp.float32)


def row_of(wide, row, rows):
    return wide[pl.ds(row, wide.shape[0] // rows, stride=rows), :]


def side_by_side(parts):
    return jnp.concatenate(parts, axis=1)


def to_grid(wide, fourier, first, rows):
    lines = [row_of(wide, first + i, rows).astype(jnp.bfloat16) for i in range(PAIR)]
    grid = dot(fourier[...], side_by_side(lines))
    return [grid[:, i * 128 : (i + 1) * 128] for i in range(PAIR)]


def to_modes(wide, turned, fields, first, rows):
    spectra = dot(turned[...], side_by_side(fields))
    for i in range(PAIR):
        wide[pl.ds(first + i, spectra.shape[0], stride=rows), :] = spectra[
            :, i * 128 : (i + 1) * 128
        ]


def network(current, w_in, w_out, low_ref, hidden_ref, moved_ref, row):
    low = current.astype(jnp.bfloat16)
    hidden = jnp.tanh(dot(low, w_in[...])).astype(jnp.bfloat16)
    moved = current + dot(hidden, w_out[...])
    low_ref[row] = low
    hidden_ref[row] = hidden
    moved_ref[row] = moved
    return moved.astype(jnp.bfloat16)


def by_pairs(rows):
    def wrapped(run):
        for first in range(0, rows, PAIR):
            run(first)

    return wrapped


def start_kernel(rows, frame, turned, w_in, w_out, spectra, moved, low, hidden, wide):
    @by_pairs(rows)
    def _(first):
        fields = [
            network(frame[row].astype(jnp.float32), w_in, w_out, low, hidden, moved, row)
            for row in range(first, first + PAIR)
        ]
        to_modes(wide, turned, fields, first, rows)

    spectra[...] = wide[...].astype(jnp.bfloat16)


def ahead_kernel(rows, last, returned, before, fourier, turned, w_in, w_out, *rest):
    if last:
        aim, spectra, moved, low, hidden, back, wide = rest
    else:
        spectra, moved, low, hidden, back, wide = rest
    back[...] = returned[...].astype(jnp.float32)

    @by_pairs(rows)
    def _(first):
        grid = to_grid(back, fourier, first, rows)
        fields = [
            network(before[first + i] - grid[i], w_in, w_out, low, hidden, moved, first + i)
            for i in range(PAIR)
        ]
        to_modes(wide, turned, fields, first, rows)

    if last:
        owners = spectra.shape[0]
        spectra[:, 0] = wide[...].astype(jnp.bfloat16).reshape(owners, -1, 128)
        spectra[:, 1] = aim[...].reshape(owners, -1, 128)
    else:
        spectra[...] = wide[...].astype(jnp.bfloat16)


def aim_kernel(rows, target, turned, spectra, wide):
    @by_pairs(rows)
    def _(first):
        to_modes(wide, turned, [target[first + i] for i in range(PAIR)], first, rows)

    spectra[...] = wide[...].astype(jnp.bfloat16)


def adjoint_kernel(rows, first_one, last, returned, base, *rest):
    rest = list(rest)
    target = rest.pop(0) if first_one else None
    low, hidden, fourier, out_t = rest[:4]
    rest = rest[4:]
    if last:
        sum_in, sum_out, sums, back, total_in, total_out = rest
    else:
        turned, in_t = rest[:2]
        rest = rest[2:]
        if first_one:
            sum_in = sum_out = None
        else:
            sum_in, sum_out = rest[:2]
            rest = rest[2:]
        spectra, adjoint, total_in, total_out, back, wide = rest
    back[...] = returned[...].astype(jnp.float32)
    if first_one:
        total_in[...] = jnp.zeros_like(total_in)
        total_out[...] = jnp.zeros_like(total_out)
    else:
        total_in[...] = sum_in[...]
        total_out[...] = sum_out[...]

    @by_pairs(rows)
    def _(first):
        grid = to_grid(back, fourier, first, rows)
        fields = []
        for i in range(PAIR):
            row = first + i
            if first_one:
                pulled = (base[row] - target[row].astype(jnp.float32) - grid[i]) * (1.0 / LAT)
            else:
                pulled = base[row] - grid[i]
            pulled_low = pulled.astype(jnp.bfloat16)
            units = hidden[row]
            total_out[...] += across(pulled_low, units)
            wide_units = units.astype(jnp.float32)
            inner = (dot(pulled_low, out_t[...]) * (1.0 - wide_units * wide_units)).astype(
                jnp.bfloat16
            )
            total_in[...] += across(low[row], inner)
            if not last:
                value = pulled + dot(inner, in_t[...])
                adjoint[row] = value
                fields.append(value.astype(jnp.bfloat16))
        if not last:
            to_modes(wide, turned, fields, first, rows)

    if last:
        height = total_in.shape[0]
        halves = total_in.shape[1] // 128
        for h in range(halves):
            part = slice(h * 128, (h + 1) * 128)
            sums[h * height : (h + 1) * height] = total_in[:, part]
            sums[(halves + h) * height : (halves + h + 1) * height] = total_out[:, part].T
    else:
        spectra[...] = wide[...].astype(jnp.bfloat16)


def parted_kernel(total, grad_in, grad_out):
    height = grad_in.shape[1]
    halves = grad_in.shape[2] // 128
    for h in range(halves):
        grad_in[0, :, h * 128 : (h + 1) * 128] = total[h * height : (h + 1) * height]
    grad_out[0] = total[halves * height :]


def gather_lines(block, k):
    values = block[:, k].astype(jnp.float32)
    owners, pair, channels = values.shape
    values = values.reshape(owners, 2, pair // 2, channels)
    return side_by_side([values[:, r].reshape(-1, channels) for r in range(2)])


def scatter_lines(out, k, values):
    owners = out.shape[0]
    halves = [values[:, r * 128 : (r + 1) * 128].reshape(owners, 1, -1, 128) for r in range(2)]
    lines = jnp.concatenate(halves, axis=1)
    out[:, k] = lines.reshape(owners, -1, 128).astype(jnp.bfloat16)


def filtered(spectra, table, turned, damping):
    coefficients = (dot(turned, spectra) * damping[...]).astype(jnp.bfloat16)
    return dot(table, coefficients)


def filter_kernel(received, table, turned, damping, out):
    @pl.loop(0, table.shape[0], step=SHARE)
    def _(first):
        for k in [first + i for i in range(SHARE)]:
            spectra = gather_lines(received, k).astype(jnp.bfloat16)
            scatter_lines(out, k, filtered(spectra, table[k], turned[k], damping))


def filter_twice_kernel(received, norms, table, turned, damping, out):
    @pl.loop(0, table.shape[0], step=SHARE)
    def _(start):
        for k in [start + i for i in range(SHARE)]:
            spectra = gather_lines(received.at[:, 0], k)
            first = filtered(spectra.astype(jnp.bfloat16), table[k], turned[k], damping)
            second = 2.0 * spectra - gather_lines(received.at[:, 1], k) - norms[k] * first
            scatter_lines(
                out, k, filtered(second.astype(jnp.bfloat16), table[k], turned[k], damping)
            )


def params(limit=VMEM):
    return pltpu.CompilerParams(vmem_limit_bytes=limit)


def shaped(shape, dtype):
    return jax.ShapeDtypeStruct(shape, dtype)


def in_smem():
    return pl.BlockSpec(memory_space=pltpu.SMEM)


def anywhere():
    return pl.BlockSpec(memory_space=pl.ANY)


def in_vmem():
    return pl.BlockSpec(memory_space=pltpu.VMEM)


def paired_kernel(first, second, after, out, slots, in_sems, out_sems):
    places = [(p, s) for p in range(2) for s in range(first.shape[0])]
    ins, outs = [], []
    for p, s in places:
        source = (first, second)[p].at[s]
        ins.append(pltpu.make_async_copy(source, slots.at[s, p], in_sems.at[p, s]))
        outs.append(pltpu.make_async_copy(slots.at[s, p], out.at[s, p], out_sems.at[p, s]))
    for copy in ins:
        copy.start()
    for copy, after in zip(ins, outs):
        copy.wait()
        after.start()
    for copy in outs:
        copy.wait()


def paired(first, second, after):
    rows = first.shape[0]
    shape = (rows, 2) + first.shape[1:]
    return pl.pallas_call(
        paired_kernel,
        in_specs=[anywhere()] * 3,
        out_specs=anywhere(),
        out_shape=shaped(shape, first.dtype),
        scratch_shapes=[
            pltpu.VMEM(shape, first.dtype),
            pltpu.SemaphoreType.DMA((2, rows)),
            pltpu.SemaphoreType.DMA((2, rows)),
        ],
        compiler_params=params(MOST),
        name="paired",
    )(first, second, after)


def chosen_kernel(window, both, frame, held):
    for k in range(frame.shape[0]):
        frame[k] = both[window[k], 0]
        held[k] = both[k, 1]


def chosen(window, both):
    members = both.shape[0]
    out = shaped((members,) + both.shape[2:], both.dtype)
    return pl.pallas_call(
        chosen_kernel,
        in_specs=[in_smem(), in_vmem()],
        out_specs=[in_vmem()] * 2,
        out_shape=[out, out],
        compiler_params=params(),
        name="chosen",
    )(jnp.clip(window, 0, members - 1), both)


def body(frames, window, targets, w_in, w_out, legendre, damping):
    rows, longitudes, channels = frames.shape[1:]
    units = w_in.shape[2]
    size_x, size_z = lax.axis_size("x"), lax.axis_size("z")
    members = lax.axis_size(MEMBER)
    owners = size_x * members
    modes = legendre.shape[0]
    degrees = legendre.shape[2]
    lines = owners * 2 * modes * rows
    width = 2 * modes * owners
    place = lax.axis_index(MEMBER)
    plane = lax.axis_index("z")
    bf16, f32 = jnp.bfloat16, jnp.float32

    swap = [
        ((x * size_z + z) * members + k, (x * size_z + k) * members + z)
        for x in range(size_x)
        for z in range(size_z)
        for k in range(members)
    ]
    first_layer = lax.ppermute(w_in[0], EVERY, swap)
    second_layer = lax.ppermute(w_out[0], EVERY, swap)

    table = lax.dynamic_index_in_dim(legendre, place, 0, keepdims=False)
    table = table.reshape(size_x, size_z, rows, degrees)
    table = table.transpose(0, 2, 1, 3).reshape(owners * rows, degrees)
    both = paired(frames[0], targets[0], table)
    table = lax.all_gather(table, "z")

    both = exchange(both, MEMBER)
    both, first_layer, second_layer = lax.optimization_barrier((both, first_layer, second_layer))
    frame, held = chosen(window, both)
    frame = exchange(frame, "z")
    held, frame, table = lax.optimization_barrier((held, frame, table))
    held = lax.all_gather(held, "z")

    table = table.reshape(modes, owners * rows, degrees)
    turned_table = table.transpose(0, 2, 1)

    ordered = np.arange(modes * owners, dtype=np.int32)
    ordered = ordered.reshape(size_x, size_z, members).transpose(0, 2, 1).reshape(-1)
    matrix = fourier_matrix(longitudes, ordered)
    fourier = jnp.asarray(matrix).astype(bf16)
    turned = jnp.asarray(np.ascontiguousarray(matrix.T)).astype(bf16)

    mode = (lax.axis_index("x") * size_z + jnp.arange(modes)) * members + place
    norms = jnp.where(mode[:, None] == 0, jnp.array([[2.0, 0.0]]), 1.0)
    norms = jnp.repeat(norms, channels, axis=1).reshape(modes, 1, 2 * channels)
    decay = jnp.broadcast_to(damping[:, None], (degrees, 2 * channels))

    shape = (rows, longitudes, channels)
    deep_shape = (rows, longitudes, units)
    buffer = pltpu.VMEM((lines, channels), f32)

    def forward(returned, before, aim=None):
        last = aim is not None
        if returned is None:
            kernel = functools.partial(start_kernel, rows)
            operands = [before, turned, first_layer, second_layer]
            scratch = [buffer]
        else:
            kernel = functools.partial(ahead_kernel, rows, last)
            operands = [returned, before, fourier, turned, first_layer, second_layer]
            operands += [aim] if last else []
            scratch = [buffer, buffer]
        cells = rows * longitudes
        return pl.pallas_call(
            kernel,
            out_shape=[
                shaped((owners, 2, lines // owners, channels) if last else (lines, channels), bf16),
                shaped(shape, f32),
                shaped(shape, bf16),
                shaped(deep_shape, bf16),
            ],
            scratch_shapes=scratch,
            compiler_params=params(),
            cost_estimate=pl.CostEstimate(
                flops=4 * cells * channels * (units + width),
                bytes_accessed=9 * cells * channels * 2,
                transcendentals=cells * units,
            ),
            name="forward",
        )(*operands)

    def transformed(target):
        return pl.pallas_call(
            functools.partial(aim_kernel, rows),
            out_shape=shaped((lines, channels), bf16),
            scratch_shapes=[buffer],
            compiler_params=params(),
            cost_estimate=pl.CostEstimate(
                flops=2 * rows * longitudes * channels * width,
                bytes_accessed=4 * lines * channels,
                transcendentals=0,
            ),
            name="aim",
        )(target, turned)

    def adjoint_of(returned, base, low, hidden, sums, target=None, last=False):
        first_one = target is not None
        operands = [returned, base] + ([target] if first_one else [])
        operands += [low, hidden, fourier, out_t]
        sum_shape = shaped(first_layer.shape, f32)
        accumulators = [pltpu.VMEM(first_layer.shape, f32)] * 2
        if last:
            operands += list(sums)
            outs = shaped((2 * units, channels), f32)
            scratch = [buffer] + accumulators
        else:
            operands += [turned, in_t] + ([] if first_one else list(sums))
            outs = [shaped((lines, channels), bf16), shaped(shape, f32), sum_shape, sum_shape]
            scratch = [buffer, buffer]
        cells = rows * longitudes
        return pl.pallas_call(
            functools.partial(adjoint_kernel, rows, first_one, last),
            out_shape=outs,
            scratch_shapes=scratch,
            compiler_params=params(),
            cost_estimate=pl.CostEstimate(
                flops=4 * cells * channels * (2 * units + width),
                bytes_accessed=11 * cells * channels * 2,
                transcendentals=0,
            ),
            name="adjoint",
        )(*operands)

    blocks = (owners, modes, 2 * rows, channels)

    def filtering(received):
        out = pl.pallas_call(
            filter_kernel,
            out_shape=shaped(blocks, bf16),
            compiler_params=params(),
            cost_estimate=pl.CostEstimate(
                flops=8 * lines * channels * degrees,
                bytes_accessed=8 * lines * channels,
                transcendentals=0,
            ),
            name="filter",
        )(received.reshape(blocks), table, turned_table, decay)
        return out.reshape(lines, channels)

    def filtering_twice(received):
        received = received.reshape(owners, 2, modes, 2 * rows, channels)
        out = pl.pallas_call(
            filter_twice_kernel,
            out_shape=shaped(blocks, bf16),
            compiler_params=params(),
            cost_estimate=pl.CostEstimate(
                flops=16 * lines * channels * degrees,
                bytes_accessed=10 * lines * channels,
                transcendentals=0,
            ),
            name="filter_twice",
        )(received, norms, table, turned_table, decay)
        return out.reshape(lines, channels)

    in_t, out_t = first_layer.T, second_layer.T
    table, turned_table, decay, norms, in_t, out_t, first_layer, second_layer, frame = (
        lax.optimization_barrier(
            (table, turned_table, decay, norms, in_t, out_t, first_layer, second_layer, frame)
        )
    )
    history = []
    moved, returned, aim = frame, None, None
    for step in range(STEPS):
        if step == STEPS - 1:
            held, returned = lax.optimization_barrier((held, returned))
            target = lax.dynamic_index_in_dim(held, plane, 1, keepdims=False)
            aim = transformed(target)
        spectra, moved, low, hidden = forward(returned, moved, aim)
        history.append((low, hidden))
        if step < STEPS - 1:
            returned = exchange(filtering(exchange(spectra, PLANE)), PLANE)
    received = exchange(spectra, PLANE)
    returned = exchange(filtering_twice(received), PLANE)

    sums = None
    adjoint = moved
    for step in reversed(range(1, STEPS)):
        low, hidden = history[step]
        spectra, adjoint, *sums = adjoint_of(
            returned, adjoint, low, hidden, sums, target if step == STEPS - 1 else None
        )
        returned = exchange(filtering(exchange(spectra, PLANE)), PLANE)
    low, hidden = history[0]
    sums = adjoint_of(returned, adjoint, low, hidden, sums, None, True)

    height = sums.shape[0] // owners
    pieces = exchange(sums, PLANE).reshape(owners, height, 128).sum(axis=0)
    around = exchange(jnp.broadcast_to(pieces[None], (size_z, height, 128)), "z")
    spread = jnp.broadcast_to(around[None], (size_x, members, height, 128))
    total = exchange(spread.reshape(-1, 128), PLANE)
    return tuple(
        pl.pallas_call(
            parted_kernel,
            out_shape=[shaped(w_in.shape, f32), shaped(w_out.shape, f32)],
            compiler_params=params(),
            name="parted",
        )(total)
    )


def solution(mesh):
    fine = Mesh(mesh.devices.reshape(4, 8, 4, 2), EVERY)
    lat, member = ("x", "z"), MEMBER
    return jax.shard_map(
        body,
        mesh=fine,
        in_specs=(
            P(member, lat, None, None),
            P(),
            P(member, lat, None, None),
            P(member, None, None),
            P(member, None, None),
            P(lat, None, None),
            P(),
        ),
        out_specs=(P(member, None, None), P(member, None, None)),
        check_vma=False,
    )
```
